512 devices in a mesh: oct: 32 (over z, core), dev: 16 (over y, x).
Axes of the slice: x: 4, y: 4, z: 16, core: 2. Of those that a mesh axis runs over, the one named last changes fastest.
Arguments:
- leaf_multipoles: float32 [32768, 512], P(('oct', 'dev')), may hold values from -6 to 6
- m2l_ops: bfloat16 [316, 96, 96], P(None, 'dev'), may hold values from -0.046875 to 0.046875
- compress: float32 [512, 96], replicated, may hold values from -0.25 to 0.25
- expand: float32 [96, 512], replicated, may hold values from -0.625 to 0.625
Outputs:
- leaf_locals: float32 [32768, 512], P(('oct', 'dev'))
The draws below stay inside these ranges and needn't reach their ends.
All inputs are finite; a program needn't handle non-finite values.
Results may differ from the reference program's by a relative error of at most 0.0029.
Values may be sent and summed in bfloat16 or wider, within the bound.
A program may use at most 64 MiB of HBM per device.

```python
import math
import jax
import jax.numpy as jnp
import numpy as np
from jax import lax

ORDER = 8
COEF = 512
RANK = 96
CUBE = 4
GX = 8
GY = 8
GZ = 8
NBOX = 32768


def steps_of(key, shape, shards, low, top_value):
    level, own = 1.0, jax.random.fold_in(key, 6)
    for dim, shards_of in shards:
        draws = jnp.exp(jax.random.uniform(jax.random.fold_in(own, dim), (shards_of,), jnp.float32, low / len(shards), top_value / len(shards)))
        level = level * jnp.repeat(draws, shape[dim] // shards_of).reshape([-1 if axis == dim else 1 for axis in range(len(shape))])
    return level


def noise(stream_key, dims, scale, reach, split=(), kind=jnp.bfloat16):
    level = steps_of(stream_key, dims, split, -0.22, 0.18) if split else 1.0
    values = jax.random.normal(stream_key, dims, jnp.float32) * scale * level
    return jnp.minimum(jnp.maximum(values, -reach), reach).astype(kind)


def setup_inputs(seed: int = 0) -> dict:
    key_of = jax.random.split(jax.random.key(seed), 5)
    return {
        "leaf_multipoles": noise(key_of[0], (NBOX, COEF), 1.0, 6.0, ((0, 512),), jnp.float32),
        "m2l_ops": noise(key_of[1], (316, RANK, RANK), (RANK * 189) ** -0.5, 0.046875, ((1, 16),)),
        "compress": noise(key_of[2], (COEF, RANK), COEF ** -0.5, 0.25, (), jnp.float32),
        "expand": noise(key_of[3], (RANK, COEF), RANK ** -0.5, 0.625, (), jnp.float32),
    }


def offset_table():
    entries = []
    for step_z in range(-3, 4):
        for step_y in range(-3, 4):
            for step_x in range(-3, 4):
                if max(abs(step_z), abs(step_y), abs(step_x)) > 1:
                    entries.append((step_z, step_y, step_x))
    return entries


def offset_lookup():
    return {offset_key: number for number, offset_key in enumerate(offset_table())}


def child_maps(node_count):
    node_ids = jnp.arange(node_count, dtype=jnp.float32)
    angles = (2.0 * node_ids + 1.0) * math.pi / (2.0 * node_count)
    points = jnp.cos(angles)
    degrees = jnp.arange(1, node_count, dtype=jnp.float32)
    parent_poly = jnp.cos(angles[:, None] * degrees[None, :])
    matrices = []
    for child_side in range(2):
        shifted = (points + (2.0 * child_side - 1.0)) / 2.0
        child_poly = jnp.cos(jnp.arccos(shifted)[:, None] * degrees[None, :])
        products = jnp.sum(parent_poly[:, None, :] * child_poly[None, :, :], axis=-1)
        matrices.append(1.0 / node_count + (2.0 / node_count) * products)
    return jnp.stack(matrices)


def transfer_maps(node_count):
    side_maps = child_maps(node_count)
    coef_count = node_count ** 3
    matrices = []
    for octant in range(8):
        along_z = side_maps[octant // 4]
        along_y = side_maps[(octant // 2) % 2]
        along_x = side_maps[octant % 2]
        tensor = along_z[:, None, None, :, None, None] * along_y[None, :, None, None, :, None] * along_x[None, None, :, None, None, :]
        matrices.append(tensor.reshape(coef_count, coef_count))
    return jnp.stack(matrices)


def upward(finer, transfer):
    size_z, size_y, size_x, coef_count = finer.shape
    grouped = finer.reshape(size_z // 2, 2, size_y // 2, 2, size_x // 2, 2, coef_count)
    grouped = grouped.transpose(1, 3, 5, 0, 2, 4, 6).reshape(8, -1, coef_count)
    parents = jnp.einsum("qnc,qdc->nd", grouped, transfer, precision=lax.Precision.HIGHEST)
    return parents.reshape(size_z // 2, size_y // 2, size_x // 2, coef_count)


def downward(coarse, transfer):
    size_z, size_y, size_x, coef_count = coarse.shape
    spread = jnp.einsum("nd,qdc->qnc", coarse.reshape(-1, coef_count), transfer, precision=lax.Precision.HIGHEST)
    spread = spread.reshape(2, 2, 2, size_z, size_y, size_x, coef_count).transpose(3, 0, 4, 1, 5, 2, 6)
    return spread.reshape(2 * size_z, 2 * size_y, 2 * size_x, coef_count)


def compress_rows(grid_values, compress):
    flat_rows = jnp.dot(grid_values.reshape(-1, grid_values.shape[-1]), compress, precision=lax.Precision.HIGHEST, preferred_element_type=jnp.float32)
    return flat_rows.astype(jnp.bfloat16).reshape(grid_values.shape[:-1] + (compress.shape[1],))


def expand_rows(grid_values, expand):
    flat_rows = jnp.dot(grid_values.reshape(-1, grid_values.shape[-1]), expand, precision=lax.Precision.HIGHEST, preferred_element_type=jnp.float32)
    return flat_rows.reshape(grid_values.shape[:-1] + (expand.shape[1],))


def pair_table():
    lookup = offset_lookup()
    entries = []
    for target in range(8):
        parity = (target // 4, (target // 2) % 2, target % 2)
        for offset_key, number in lookup.items():
            shifted = [parity[axis_id] + offset_key[axis_id] + 3 for axis_id in range(3)]
            if min(shifted) >= 1 and max(shifted) <= 6:
                phase_id = (shifted[0] % 2) * 4 + (shifted[1] % 2) * 2 + shifted[2] % 2
                entries.append((target, phase_id, shifted[0] // 2, shifted[1] // 2, shifted[2] // 2, number))
    return np.array(entries, dtype=np.int32)


def interactions(packed, m2l_ops):
    size_z, size_y, size_x, rank_count = packed.shape
    even_z, even_y, even_x = size_z + size_z % 2, size_y + size_y % 2, size_x + size_x % 2
    padded = jnp.pad(packed, ((3, 3 + even_z - size_z), (3, 3 + even_y - size_y), (3, 3 + even_x - size_x), (0, 0)))
    phases = padded.reshape((even_z + 6) // 2, 2, (even_y + 6) // 2, 2, (even_x + 6) // 2, 2, rank_count)
    phases = phases.transpose(1, 3, 5, 0, 2, 4, 6).reshape(8, (even_z + 6) // 2, (even_y + 6) // 2, (even_x + 6) // 2, rank_count)
    half_z, half_y, half_x = even_z // 2, even_y // 2, even_x // 2
    pair_rows = jnp.asarray(pair_table())
    anchor = jnp.zeros((), jnp.int32)

    def accumulate(pair_index, totals):
        entry_row = pair_rows[pair_index]
        window = lax.dynamic_slice(phases, (entry_row[1], entry_row[2], entry_row[3], entry_row[4], anchor), (1, half_z, half_y, half_x, rank_count))
        contribution = jnp.dot(window.reshape(-1, rank_count), m2l_ops[entry_row[5]], preferred_element_type=jnp.float32)
        current = lax.dynamic_slice(totals, (entry_row[0], anchor, anchor), (1, half_z * half_y * half_x, rank_count))
        return lax.dynamic_update_slice(totals, current + contribution[None], (entry_row[0], anchor, anchor))

    totals = jnp.zeros((8, half_z * half_y * half_x, rank_count), jnp.float32)
    totals = lax.fori_loop(0, pair_rows.shape[0], accumulate, totals)
    totals = totals.reshape(2, 2, 2, half_z, half_y, half_x, rank_count).transpose(3, 0, 4, 1, 5, 2, 6)
    return totals.reshape(even_z, even_y, even_x, rank_count)[:size_z, :size_y, :size_x]


def reference(leaf_multipoles, m2l_ops, compress, expand):
    transfer = transfer_maps(ORDER)
    finest = leaf_multipoles.reshape(GZ, GY, GX, CUBE, CUBE, CUBE, COEF)
    finest = finest.transpose(0, 3, 1, 4, 2, 5, 6).reshape(GZ * CUBE, GY * CUBE, GX * CUBE, COEF)
    levels = [finest]
    for level_id in range(3):
        levels.append(upward(levels[-1], transfer))
    local_field = None
    for level_id in range(3, -1, -1):
        packed = compress_rows(levels[level_id], compress)
        gathered = interactions(packed, m2l_ops) * (0.5 ** level_id)
        incoming = expand_rows(gathered, expand)
        if level_id == 3:
            local_field = incoming
        else:
            local_field = downward(local_field, transfer) + incoming
    local_field = local_field.reshape(GZ, CUBE, GY, CUBE, GX, CUBE, COEF).transpose(0, 2, 4, 1, 3, 5, 6)
    return local_field.reshape(-1, COEF)
```

```python
import math

import jax
import jax.numpy as jnp
import numpy as np
from jax import lax
from jax.experimental import pallas as pl
from jax.experimental.pallas import tpu as pltpu
from jax.sharding import PartitionSpec as P


F32 = jnp.float32
BF16 = jnp.bfloat16
MESH = pl.DeviceIdType.MESH
TOPS = 48


def side_maps():
    ids = np.arange(8, dtype=np.float64)
    angles = (2 * ids + 1) * math.pi / 16
    points = np.cos(angles)
    degrees = np.arange(1, 8, dtype=np.float64)
    parent = np.cos(angles[:, None] * degrees[None, :])
    maps = []
    for side in range(2):
        child = np.cos(np.arccos((points + 2 * side - 1) / 2)[:, None] * degrees[None, :])
        maps.append(1 / 8 + 2 / 8 * parent @ child.T)
    return np.stack(maps)


def octant(number):
    return number // 4, number // 2 % 2, number % 2


def tables():
    side = side_maps()
    t = {}
    leaf_order = np.zeros((64, 64))
    up_five = np.zeros((8, 8, 8, 2, 8))
    for box in range(64):
        a, b, c = box // 16, box // 4 % 4, box % 4
        parent = (a // 2) * 4 + (b // 2) * 2 + c // 2
        leaf_order[((b % 2) * 2 + c % 2) * 16 + (a % 2) * 8 + parent, box] = 1
        up_five[:, parent, :, a % 2, parent] = side[a % 2]
    t["leaf_order"] = leaf_order
    pair = np.zeros((2, 2, 8, 8, 8, 8))
    for qy in range(2):
        for qx in range(2):
            pair[qy, qx] = np.einsum("ab,cd->bdac", side[qy], side[qx])
    t["pair_up"] = pair.reshape(256, 64)
    twice = np.stack([side[a // 2] @ side[a % 2] for a in range(4)])
    zmaps, planes = [], []
    for own in range(2):
        upper = np.stack([twice, side[own] @ twice])
        up = np.zeros((2, 4, 8, 8, 2, 8))
        down = np.zeros((2, 8, 8, 128))
        for box in range(8):
            lz, rest = box // 4, box % 4
            for qz in range(2):
                for level in range(2):
                    up[level, rest, :, :, qz, box] = upper[level, 2 * lz + qz]
                    start = 64 + 32 * level + 8 * rest
                    down[qz, :, box, start : start + 8] = upper[level, 2 * lz + qz].T
                for node in range(8):
                    down[qz, :, box, node * 8 + box] = side[qz][node]
        up = np.concatenate([up_five.reshape(64, 128), up.reshape(64, 128)])
        zmaps.append(np.concatenate([halved(up), halved(down.reshape(128, 128))]))
    for own in range(4):
        plane = np.zeros((2, 2, 2, 2, 8, 8, 2, 8, 8))
        for ly, lx, qy, qx in np.ndindex(2, 2, 2, 2):
            first, second = twice[2 * ly + qy], twice[2 * lx + qx]
            plane[ly, lx, qy, qx, :, :, 0] = np.einsum("ab,cd->bdac", first, second)
            plane[ly, lx, qy, qx, :, :, 1] = np.einsum("ab,cd->bdac", side[own // 2] @ first, side[own % 2] @ second)
        planes.append(halved(plane.reshape(1024, 128)))
    t["zmaps"] = np.stack(zmaps)
    t["planes"] = np.stack(planes)
    spread = np.zeros((96, 128))
    for rank in range(96):
        spread[rank, rank // 6 * 8 + rank % 6] = 1
    t["spread"] = spread
    gather = np.zeros((2, 2, 4, 16, 128))
    shift = np.zeros((3, 8, 16, 8, 16))
    lanes = np.zeros((2, 3, 128, 256))
    for pz in range(2):
        for py in range(4):
            for px in range(16):
                source = (py // 2) * 8 + px // 2
                gather[0, pz, py, px, source * 8 + pz * 4 + (py % 2) * 2 + px % 2] = 1
                if py in (0, 3) and px < 8:
                    gather[1, pz, py, px, ((py == 3) * 8 + px) * 8] = 1
    for wx in range(3):
        for px in range(16):
            if 0 <= px + wx - 1 < 16:
                for block in range(8):
                    shift[wx, block, px, block, px + wx - 1] = 1
        for phase in range(8):
            for r in range(8):
                place = phase // 2 * 64 + r * 8 + 1 + 2 * wx + phase % 2
                lanes[0, wx, phase * 8 + r, place] = 1
                lanes[1, wx, 64 + phase * 8 + r, place] = 1
    t["gather"] = np.concatenate([gather.reshape(256, 128), shift.reshape(384, 128)])
    t["lanes"] = lanes.reshape(2, 384, 256)
    sel_three = np.zeros((256, 512))
    for gy in range(2):
        for px in range(4):
            for node in range(1, 7):
                gx = 2 * px - 3 + node
                if 0 <= gx < 8:
                    for r in range(8):
                        sel_three[gy * 128 + 64 + gx * 8 + r, px * 128 + gy * 64 + r * 8 + node] = 1
    t["sel_three"] = sel_three
    sel_two = np.zeros((128, 512))
    for px in range(2):
        for fy in range(2):
            for node in range(1, 7):
                bx = 2 * px - 3 + node
                if 0 <= bx < 4:
                    for r in range(8):
                        sel_two[64 + bx * 8 + r, (px * 2 + fy) * 128 + fy * 64 + r * 8 + node] = 1
    t["sel_two"] = sel_two
    back = np.zeros((16, 16, 256))
    for source in range(16):
        for lp in range(8):
            lz, ly, lx = octant(lp)
            row = lz * 64 + ((source // 8) * 2 + ly) * 16 + (source % 8) * 2 + lx
            back[source, lp, row] = 1
            back[source, 8 + lp, 128 + row] = 1
    t["back"] = back.reshape(256, 256)
    choose = np.zeros((49, 8, 316))
    number = 0
    for cell in range(49):
        for x in range(7):
            if max(abs(cell // 7 - 3), abs(cell % 7 - 3), abs(x - 3)) > 1:
                choose[cell, x, number] = 1
                number += 1
    t["choose"] = choose.reshape(392, 316)
    return t


def top_rows(levels_z):
    table = np.zeros((levels_z // 2, 4, 9, 2, 8, 256))
    for half in range(levels_z // 2):
        for k in range(4):
            for block in range(9):
                for fz in range(2):
                    z = 2 * (half + block // 3 - 1) + fz
                    y = k + block % 3 - 1
                    if 0 <= z < levels_z and 0 <= y < 4:
                        for px in range(4):
                            table[half, k, block, fz, px, px * 32 + z * 4 + y] = 1
                    z = 2 * (half // 2 + block // 3 - 1) + fz
                    for fy in range(2):
                        y = 2 * (k // 2 + block % 3 - 1) + fy
                        if 0 <= z < levels_z // 2 and 0 <= y < 4:
                            for px in range(2):
                                table[half, k, block, fz, 4 + px, 128 + (px * 2 + fy) * 16 + z * 4 + y] = 1
    return table.reshape(levels_z // 2 * 4, 144, 256)[:, :, :192]


def back_tops():
    table = np.zeros((4, 2, 16, 16, 8, TOPS))
    for gz in range(4):
        for k in range(2):
            for source in range(16):
                gy, gx = source // 8, source % 8
                for q in range(8):
                    table[gz, k, source, q, q, gy * 16 + gx] = 1
                table[gz, k, source, 8, gz % 2 * 4 + gy * 2 + gx % 2, 32 + gx // 2] = 1
                table[gz, k, source, 9, gz // 2 * 4 + k * 2 + gx // 2 % 2, 36 + gx // 4] = 1
    return table.reshape(8, 256, 8 * TOPS)


def split(value):
    if isinstance(value, tuple):
        return value
    high = value.astype(BF16)
    return high, (value - high.astype(F32)).astype(BF16)


def fdot(a, b, turned=False):
    (a_high, a_low), (b_high, b_low) = split(a), split(b)
    return bdot(a_high, b_high, turned) + (bdot(a_high, b_low, turned) + bdot(a_low, b_high, turned))


def bdot(a, b, turned=False):
    return lax.dot_general(a, b, (((1,), (1 if turned else 0,)), ((), ())), preferred_element_type=F32)


def rows_to_lanes(value, count):
    rows = value.shape[0] // count
    return jnp.concatenate([value[rows * n : rows * n + rows] for n in range(count)], axis=1)


def lanes_to_rows(value, count):
    width = value.shape[1] // count
    return jnp.concatenate([value[:, width * n : width * n + width] for n in range(count)], axis=0)


def upward(leaves, spread, c):
    order = c("leaf_order")[0]
    parts = [bdot(order, part) for part in split(leaves)]
    mixed = []
    for part in parts:
        lines = []
        for node in range(8):
            lines.append(
                jnp.concatenate([part[16 * n : 16 * n + 16, 64 * node : 64 * node + 64] for n in range(4)], axis=1)
            )
        mixed.append(jnp.concatenate(lines, axis=0).astype(BF16))
    mixed = fdot(c("up"), tuple(mixed))
    four = fdot(mixed[:64], c("pair_up"))
    upper = jnp.concatenate([rows_to_lanes(mixed[64:96], 4), rows_to_lanes(mixed[96:], 4)], axis=0)
    upper = fdot(upper, c("planes"))
    three, two = upper[:8, :64], upper[8:, 64:]
    rest = jnp.concatenate(
        [rows_to_lanes(four, 8), rows_to_lanes(three, 8), rows_to_lanes(two, 8), jnp.zeros((6, 512), F32)], axis=0
    )
    every = [jnp.concatenate([part.astype(BF16), extra], axis=0) for part, extra in zip(parts, split(rest))]
    return fdot(tuple(every), spread, turned=True)


def spread_ranks(turned_compress, c):
    return tuple(bdot(c("spread")[0], part).astype(BF16) for part in split(turned_compress))


def messages(packed, roll):
    tiles = []
    for q in range(8):
        first = q % 4 * 16 + q // 4 * 8
        tiles.append(packed[first : first + 8])
    for q in range(8):
        lines = [packed[64 + q : 65 + q]] + ([packed[72:73], packed[73:74]] if q == 0 else [])
        tiles.append(jnp.concatenate(lines + [jnp.zeros((8 - len(lines), 128), F32)], axis=0))
    lane = lax.broadcasted_iota(jnp.int32, (8, 128), 1)
    for bit in (1, 2, 4, 8):
        upper = lane // 8 // bit % 2 == 1
        for n in range(16):
            if n & bit == 0:
                low, high = tiles[n], tiles[n | bit]
                tiles[n] = jnp.where(upper, roll(high, 8 * bit, 1), low)
                tiles[n | bit] = jnp.where(upper, high, roll(low, 128 - 8 * bit, 1))
    return tiles


def top_row(tiles, roll):
    lane = lax.broadcasted_iota(jnp.int32, (8, 128), 1)
    mask = lane // 8 == 8
    sums = [jnp.zeros((8, 128), F32) for _ in range(3)]
    for n in range(16):
        kept = jnp.where(mask, tiles[n], 0.0)
        gx = n % 8
        sums[n // 8] += roll(kept, 8 * gx, 1) if gx else kept
        sums[2] += roll(kept, 8 * (gx // 2), 1) if gx // 2 else kept
    return jnp.concatenate([sums[0][1:2], sums[1][1:2], sums[2][2:3]], axis=1)


def assemble(received, c):
    picked = bdot(c("gather"), received.astype(BF16))
    lane = lax.broadcasted_iota(jnp.int32, (128, 128), 1)
    return jnp.where(lane < 64, picked[:128], picked[128:]).astype(BF16)


def widen(raw, blocks, five, four, c):
    narrow = jnp.concatenate([raw[z, y] for z, y in blocks], axis=0)
    wide, fours = [], []
    for start in range(0, len(blocks), 8):
        shifted = bdot(c("shift"), narrow[16 * start : 16 * start + 128]).astype(BF16)
        wide.append(rows_to_lanes(shifted, 3))
    wide = jnp.concatenate(wide, axis=0)
    result = bdot(wide, c("lanes_five")).astype(BF16)
    for n, (z, y) in enumerate(blocks):
        five[z, y] = result[16 * n : 16 * n + 16]
        if z in (0, 1, 3) and y in (0, 1, 4, 5):
            fours.append((n, (0, 1, 3).index(z), (0, 1, 4, 5).index(y)))
    result = bdot(jnp.concatenate([wide[16 * n : 16 * n + 16] for n, _, _ in fours], axis=0), c("lanes_four"))
    for place, (_, z, y) in enumerate(fours):
        four[z, y] = result[16 * place : 16 * place + 16].astype(BF16)


OWN = [(z, y) for z in (1, 2) for y in range(1, 5)]
AROUND = [(z, y) for z in range(4) for y in range(6) if (z, y) not in OWN]


def top_blocks(rows, pick, c):
    three = jnp.concatenate([row[:, :256] for row in rows], axis=0).astype(BF16)
    pairs = []
    for n in range(16):
        first = n // 4 * 8 + n % 4
        pairs.append(rows[first][:, 256:] + rows[first + 4][:, 256:])
    two = jnp.concatenate(pairs, axis=0).astype(BF16)
    stacked = jnp.concatenate(
        [
            lanes_to_rows(bdot(three, c("sel_three")), 4),
            lanes_to_rows(bdot(two, c("sel_two")), 4),
        ],
        axis=0,
    ).astype(BF16)
    return bdot(pick, stacked)


def lift_up(summed):
    total = summed[0].astype(F32)
    for n in range(1, 16):
        total = total + summed[n].astype(F32)
    return total


def down_top(summed, expand, c):
    row = lax.broadcasted_iota(jnp.int32, (16, 128), 0)
    scale = jnp.where(row < 8, 0.5, jnp.where(row == 8, 0.25, 0.125))
    fields = fdot((summed * scale)[:, :96], expand)
    two, three = lanes_to_rows(fields[9:10], 8), lanes_to_rows(fields[8:9], 8)
    zero = jnp.zeros((8, 64), F32)
    upper = jnp.concatenate(
        [jnp.concatenate([three, zero], axis=1), jnp.concatenate([zero, two], axis=1)], axis=0
    )
    upper = fdot(upper, c("planes"), turned=True)
    four = fdot(lanes_to_rows(fields[:8], 8), c("pair_up"), turned=True)
    five = fdot(
        c("down"),
        jnp.concatenate([four, lanes_to_rows(upper[:8], 4), lanes_to_rows(upper[8:], 4)], axis=0),
    )
    results = []
    for q in range(8):
        part = five[q // 4 * 64 : q // 4 * 64 + 64, q % 4 * 64 : q % 4 * 64 + 64]
        results.append(rows_to_lanes(part, 8))
    return jnp.concatenate(results, axis=0)


def expand_five(summed, expand):
    parts = []
    for q in range(8):
        pz, lane = q // 4, 128 * (q % 4)
        parts.append(summed[8 * pz : 8 * pz + 8, lane : lane + 128])
    return fdot(jnp.concatenate(parts, axis=0)[:, :96], expand)


def down_five(result, lines, out_ref):
    for q in range(8):
        qz, qy, qx = octant(q)
        for lz in range(2):
            for ly in range(2):
                first = lz * 32 + qz * 16 + ly * 8 + qy * 4 + qx
                source = q * 8 + lz * 4 + ly * 2
                for n in range(4):
                    lines[n, pl.ds(first, 2, stride=2), :] = result[source : source + 2, 128 * n : 128 * n + 128]
    for n in range(4):
        out_ref[:, 128 * n : 128 * n + 128] = lines[n]


PAIRS = {"leaf_order": (64, 64), "spread": (128, 96), "pair_up": (256, 64)}
NARROW = {"lanes_five": 384, "lanes_four": 384, "back": 256}
SELECT = {"sel_three": 256, "sel_two": 128}


def places(sizes):
    start, found = 0, {}
    for name, rows in sizes.items():
        found[name] = start, rows
        start += -(-rows // 16) * 16
    return found, start


PAIR_PLACES, PAIR_ROWS = places({name: shape[0] for name, shape in PAIRS.items()})
NARROW_PLACES, NARROW_ROWS = places(NARROW)
SELECT_PLACES, SELECT_ROWS = places(SELECT)


def halved(value):
    value = value.astype(np.float32)
    high = value.astype(jnp.bfloat16)
    return np.stack([high, (value - high.astype(np.float32)).astype(jnp.bfloat16)])


def packed_tables(groups):
    t = tables()
    t["lanes_five"], t["lanes_four"] = t["lanes"]
    t["spread"] = t["spread"].T
    pairs = np.zeros((PAIR_ROWS, 128))
    for name, (start, rows) in PAIR_PLACES.items():
        pairs[start : start + rows, : PAIRS[name][1]] = t[name]
    narrow = np.zeros((NARROW_ROWS, 256))
    for name, (start, rows) in NARROW_PLACES.items():
        narrow[start : start + rows] = t[name]
    select = np.zeros((SELECT_ROWS, 512))
    for name, (start, rows) in SELECT_PLACES.items():
        select[start : start + rows] = t[name]
    short = lambda value: value.astype(jnp.bfloat16)
    return [
        halved(pairs), short(t["choose"]), short(t["gather"]), short(narrow), short(select),
        t["zmaps"], t["planes"], short(top_rows(groups // 4)), short(back_tops()),
    ]


def getter(pairs, gather, narrow, select, zmaps, planes):
    def get(name):
        if name in ("up", "down"):
            start = 0 if name == "up" else 2
            return zmaps[start], zmaps[start + 1]
        if name == "planes":
            return planes[0], planes[1]
        if name == "gather":
            return gather[0:256]
        if name == "shift":
            return gather[256:640]
        if name in PAIRS:
            start, rows = PAIR_PLACES[name]
            lanes = PAIRS[name][1]
            return tuple(pairs[half, start : start + rows, 0:lanes] for half in range(2))
        if name in NARROW:
            start, rows = NARROW_PLACES[name]
            return narrow[start : start + rows]
        start, rows = SELECT_PLACES[name]
        return select[start : start + rows]

    return get


def place_transfers(m2l, choose, weights, roll):
    for rank in range(0, 8, 2):
        if rank == 6:
            weights[:, 48:64, :] = jnp.zeros((49, 16, 256), BF16)
            continue
        sides = [[], []]
        for n in (rank, rank + 1):
            rows = jnp.concatenate([m2l[n], jnp.zeros((32, 316), BF16)], axis=0)
            low = bdot(choose[0:280, 0:256], rows[:, 0:256], turned=True)
            high = bdot(choose[280:392, 128:316], rows[:, 128:316], turned=True)
            value = jnp.concatenate([low, high], axis=0)
            sides[0].append(value.reshape(49, 8, 128))
            sides[1].append(roll(value, 1, 0).reshape(49, 8, 128))
        for px in range(2):
            both = jnp.concatenate(sides[px], axis=1).astype(BF16)
            weights[:, 8 * rank : 8 * rank + 16, 128 * px : 128 * px + 128] = both


def block_transfers(weights, pz, py, block):
    wz, wy = block // 3, block % 3
    cells = [(2 * wz + fz + 1 - pz) * 7 + 2 * wy + fy + 1 - py for fz in range(2) for fy in range(2)]
    return jnp.concatenate([weights[cell] for cell in cells], axis=0)


def far_tops(four, top_ref, weights, back_top):
    lefts = []
    for block in range(9):
        wz, wy = block // 3, block % 3
        fz_parts = [top_ref[16 * block + 8 * fz : 16 * block + 8 * fz + 8, :] for fz in range(2)]
        tops = jnp.concatenate([jnp.concatenate(fz_parts, axis=1), jnp.zeros((8, 256), F32)], axis=0)
        lefts.append(jnp.concatenate([four[wz, wy : wy + 2].reshape(32, 256), tops.astype(BF16)], axis=0))
    pieces = []
    for child in range(4):
        value = None
        for block in range(9):
            product = bdot(lefts[block], block_transfers(weights, child // 2, child % 2, block))
            value = product if value is None else value + product
        short = value.astype(BF16)
        pieces += [short[:, :128], short[:, 128:]]
    return bdot(back_top, jnp.concatenate(pieces, axis=0)).astype(BF16)


def far_five(five, weights, back, py):
    values = []
    for pz in range(2):
        value = None
        for block in range(9):
            wz, wy = block // 3, block % 3
            left = five[wz : wz + 2, wy : wy + 4].reshape(128, 256)
            product = bdot(left, block_transfers(weights, pz, py, block))
            value = product if value is None else value + product
        values.append(value.astype(BF16))
    return bdot(back, jnp.concatenate(values, axis=0)).astype(BF16)


DIRECTIONS = [(dz, dk) for dz in (-1, 0, 1) for dk in (-1, 0, 1) if (dz, dk) != (0, 0)]


def halo_ranges(step, size):
    if step == 0:
        return pl.ds(1, size), pl.ds(1, size)
    if step == 1:
        return pl.ds(size, 1), pl.ds(0, 1)
    return pl.ds(1, 1), pl.ds(size + 1, 1)


def kernel(groups, *refs):
    sources, out_ref, scratch = refs[:13], refs[13], refs[14:]
    (
        leaf, m2l, compress, expand, pairs, choose, gather, narrow, select, zmaps, planes, pick, back_top,
        weights, message, received, row_ref, raw, five, four, top_ref, reply_top, reply_five, answer_top, answer_five,
        lines, load, send_a, recv_a, send_t, recv_t, send_halo, recv_halo, send_d, recv_d,
    ) = scratch
    o, v = lax.axis_index("oct"), lax.axis_index("dev")
    gz, k, gy, gx = o // 4, o % 4, v // 8, v % 8
    roll = pltpu.roll
    c = getter(pairs, gather, narrow, select, zmaps, planes)

    loads = {}
    for n, target in enumerate(scratch[:13]):
        source = sources[n]
        if target is zmaps:
            source = source.at[gz % 2]
        if target is planes:
            source = source.at[gy % 2 * 2 + gx % 2]
        if target is pick:
            source = source.at[gz // 2 * 4 + k]
        if target is back_top:
            source = source.at[gz % 4 * 2 + k % 2]
        loads[n] = pltpu.make_async_copy(source, target, load.at[n])
    for n in (0, 4, 9, 10, 2):
        loads[n].start()

    raw[...] = jnp.zeros(raw.shape, BF16)
    barrier = pltpu.get_barrier_semaphore()
    layers = groups // 4
    partners = [(n, 0) for n in range(1, layers)] + [(0, n) for n in range(1, 4)]
    partners += [(dz % layers, dk % 4) for dz in (-1, 1) for dk in (-1, 1)]
    for dz, dk in partners:
        target = lax.rem(gz + dz, layers) * 4 + lax.rem(k + dk, 4)
        pl.semaphore_signal(barrier, inc=1, device_id=(target, v), device_id_type=MESH)
    for n in range(1, 16):
        pl.semaphore_signal(barrier, inc=1, device_id=(o, lax.rem(v + n, 16)), device_id_type=MESH)
    for n in (1, 5, 6, 7, 8, 11, 12, 3):
        loads[n].start()

    for n in (0, 4, 9, 10, 2):
        loads[n].wait()
    packed = upward(leaf[...], spread_ranks(compress[...], c), c)
    tiles = messages(packed, roll)
    for n in range(16):
        message[n] = tiles[n]
    received[v] = message[v]
    pl.semaphore_wait(barrier, 15 + len(partners))

    def across(source, target, sems, n):
        return pltpu.make_async_remote_copy(
            src_ref=source.at[lax.rem(v + n, 16)], dst_ref=target.at[v], send_sem=sems[0], recv_sem=sems[1],
            device_id=(o, lax.rem(v + n, 16)), device_id_type=MESH,
        )

    def along_k(n):
        return pltpu.make_async_remote_copy(
            src_ref=row_ref.at[pl.ds(o, 1)], dst_ref=row_ref.at[pl.ds(o, 1)],
            send_sem=send_t.at[0], recv_sem=recv_t.at[0],
            device_id=(gz * 4 + lax.rem(k + n, 4), v), device_id_type=MESH,
        )

    def along_z(n):
        return pltpu.make_async_remote_copy(
            src_ref=row_ref.at[pl.ds(gz * 4, 4)], dst_ref=row_ref.at[pl.ds(gz * 4, 4)],
            send_sem=send_t.at[1], recv_sem=recv_t.at[1],
            device_id=(lax.rem(gz + n, layers) * 4 + k, v), device_id_type=MESH,
        )

    def whole(source, target, count, sems):
        return pltpu.make_async_remote_copy(
            src_ref=source.at[pl.ds(0, count)], dst_ref=target.at[pl.ds(0, count)], send_sem=sems[0], recv_sem=sems[1],
            device_id=(o, lax.rem(v + 1, 16)), device_id_type=MESH,
        )

    sems_a = (send_a, recv_a)
    for n in range(1, 16):
        across(message, received, sems_a, n).start()
    for n in (1, 5, 6, 7, 8, 11, 12, 3):
        loads[n].wait()
    place_transfers(m2l, choose, weights, roll)
    whole(message, received, 15, sems_a).wait_recv()

    got = [received[n] for n in range(16)]
    row_ref[o] = top_row(got, roll)
    for n in range(1, 4):
        along_k(n).start()
    raw[1:3, 1:5] = assemble(jnp.concatenate(got, axis=0), c).reshape(2, 4, 16, 128)

    def halo(number, dz, dk, sign):
        from_z, to_z = halo_ranges(dz, 2)
        from_y, to_y = halo_ranges(dk, 4)
        return pltpu.make_async_remote_copy(
            src_ref=raw.at[from_z, from_y], dst_ref=raw.at[to_z, to_y],
            send_sem=send_halo.at[number], recv_sem=recv_halo.at[number],
            device_id=((gz + sign * dz) * 4 + k + sign * dk, v), device_id_type=MESH,
        )

    def inside(dz, dk):
        return (gz + dz >= 0) & (gz + dz < groups // 4) & (k + dk >= 0) & (k + dk < 4)

    for number, (dz, dk) in enumerate(DIRECTIONS):
        @pl.when(inside(dz, dk))
        def _():
            halo(number, dz, dk, 1).start()

    def rows_of(step):
        return whole(row_ref, row_ref, (3, groups - 4)[step], (send_t.at[step], recv_t.at[step]))

    rows_of(0).wait_recv()
    for n in range(1, layers):
        along_z(n).start()

    widen(raw, OWN, five, four, c)

    for number, (dz, dk) in enumerate(DIRECTIONS):
        @pl.when(inside(-dz, -dk))
        def _():
            halo(number, dz, dk, -1).wait_recv()

    widen(raw, AROUND, five, four, c)
    returned_five = (reply_five, answer_five, (send_d.at[0], recv_d.at[0]))
    returned_top = (reply_top, answer_top, (send_d.at[1], recv_d.at[1]))
    for py in range(2):
        part = far_five(five, weights, c("back"), py).reshape(16, 16, 256)
        reply_five[:, :, 256 * py : 256 * py + 256] = part
    answer_five[v] = reply_five[v]
    for n in range(1, 16):
        across(*returned_five, n).start()

    rows_of(1).wait_recv()
    rows = [row_ref[n] for n in range(groups)]
    top_ref[...] = top_blocks(rows, pick[...], c)
    reply_top[...] = far_tops(four, top_ref, weights, back_top[...]).reshape(16, 16, 128)
    answer_top[v] = reply_top[v]
    for n in range(1, 16):
        across(*returned_top, n).start()

    split_expand = split(expand[...])
    whole(*returned_five[:2], 15, returned_five[2]).wait_recv()
    low = expand_five(lift_up(answer_five), split_expand)
    whole(message, received, 15, sems_a).wait_send()
    for number, (dz, dk) in enumerate(DIRECTIONS):
        @pl.when(inside(dz, dk))
        def _():
            halo(number, dz, dk, 1).wait_send()

    whole(*returned_top[:2], 15, returned_top[2]).wait_recv()
    above = down_top(lift_up(answer_top), split_expand, c)
    down_five(low + above, lines, out_ref)
    for source, target, sems in (returned_five, returned_top):
        whole(source, target, 15, sems).wait_send()
    for step in range(2):
        rows_of(step).wait_send()


def on_device(groups, leaf_multipoles, m2l_ops, compress, expand):
    values = [leaf_multipoles, m2l_ops.transpose(1, 2, 0), compress.T, expand]
    values += [jnp.asarray(value) for value in packed_tables(groups)]
    dma = pltpu.SemaphoreType.DMA
    loaded = [pltpu.VMEM(value.shape, value.dtype) for value in values[:-4]]
    loaded += [pltpu.VMEM(value.shape[1:], value.dtype) for value in values[-4:]]
    return pl.pallas_call(
        lambda *refs: kernel(groups, *refs),
        out_shape=jax.ShapeDtypeStruct((64, 512), F32),
        in_specs=[pl.BlockSpec(memory_space=pltpu.HBM)] * len(values),
        out_specs=pl.BlockSpec(memory_space=pltpu.VMEM),
        scratch_shapes=loaded
        + [
            pltpu.VMEM((49, 64, 256), BF16),
            pltpu.VMEM((16, 8, 128), F32),
            pltpu.VMEM((16, 8, 128), F32),
            pltpu.VMEM((groups, 1, 384), F32),
            pltpu.VMEM((4, 6, 16, 128), BF16),
            pltpu.VMEM((4, 6, 16, 256), BF16),
            pltpu.VMEM((3, 4, 16, 256), BF16),
            pltpu.VMEM((144, 128), F32),
            pltpu.VMEM((16, 16, 128), BF16),
            pltpu.VMEM((16, 16, 512), BF16),
            pltpu.VMEM((16, 16, 128), BF16),
            pltpu.VMEM((16, 16, 512), BF16),
            pltpu.VMEM((4, 64, 128), F32),
            dma((13,)),
            dma, dma, dma((2,)), dma((2,)), dma((8,)), dma((8,)), dma((2,)), dma((2,)),
        ],
        compiler_params=pltpu.CompilerParams(
            collective_id=0, has_side_effects=True, vmem_limit_bytes=60 * 1024 * 1024
        ),
        cost_estimate=pl.CostEstimate(flops=1_000_000_000, bytes_accessed=6_000_000, transcendentals=0),
    )(*values)


def solution(mesh):
    groups = mesh.shape["oct"]
    placed = (P(("oct", "dev"), None), P(None, "dev", None), P(), P())
    return jax.shard_map(
        lambda *args: on_device(groups, *args),
        mesh=mesh, in_specs=placed, out_specs=P(("oct", "dev"), None), check_vma=False,
    )
```

```python
import math

import jax
import jax.numpy as jnp
import numpy as np
from jax import lax
from jax.experimental import pallas as pl
from jax.experimental.pallas import tpu as pltpu
from jax.sharding import PartitionSpec as P


F32 = jnp.float32
BF16 = jnp.bfloat16
MESH = pl.DeviceIdType.MESH
TOPS = 48


def side_maps():
    ids = np.arange(8, dtype=np.float64)
    angles = (2 * ids + 1) * math.pi / 16
    points = np.cos(angles)
    degrees = np.arange(1, 8, dtype=np.float64)
    parent = np.cos(angles[:, None] * degrees[None, :])
    maps = []
    for side in range(2):
        child = np.cos(np.arccos((points + 2 * side - 1) / 2)[:, None] * degrees[None, :])
        maps.append(1 / 8 + 2 / 8 * parent @ child.T)
    return np.stack(maps)


def octant(number):
    return number // 4, number // 2 % 2, number % 2


def tables():
    side = side_maps()
    t = {}
    leaf_order = np.zeros((64, 64))
    up_five = np.zeros((8, 8, 8, 2, 8))
    for box in range(64):
        a, b, c = box // 16, box // 4 % 4, box % 4
        parent = (a // 2) * 4 + (b // 2) * 2 + c // 2
        leaf_order[((b % 2) * 2 + c % 2) * 16 + (a % 2) * 8 + parent, box] = 1
        up_five[:, parent, :, a % 2, parent] = side[a % 2]
    t["leaf_order"] = leaf_order
    pair = np.zeros((2, 2, 8, 8, 8, 8))
    for qy in range(2):
        for qx in range(2):
            pair[qy, qx] = np.einsum("ab,cd->bdac", side[qy], side[qx])
    t["pair_up"] = pair.reshape(256, 64)
    twice = np.stack([side[a // 2] @ side[a % 2] for a in range(4)])
    zmaps, planes = [], []
    for own in range(2):
        upper = np.stack([twice, side[own] @ twice])
        up = np.zeros((2, 4, 8, 8, 2, 8))
        down = np.zeros((2, 8, 8, 128))
        for box in range(8):
            lz, rest = box // 4, box % 4
            for qz in range(2):
                for level in range(2):
                    up[level, rest, :, :, qz, box] = upper[level, 2 * lz + qz]
                    start = 64 + 32 * level + 8 * rest
                    down[qz, :, box, start : start + 8] = upper[level, 2 * lz + qz].T
                for node in range(8):
                    down[qz, :, box, node * 8 + box] = side[qz][node]
        up = np.concatenate([up_five.reshape(64, 128), up.reshape(64, 128)])
        zmaps.append(np.concatenate([halved(up), halved(down.reshape(128, 128))]))
    for own in range(4):
        plane = np.zeros((2, 2, 2, 2, 8, 8, 2, 8, 8))
        for ly, lx, qy, qx in np.ndindex(2, 2, 2, 2):
            first, second = twice[2 * ly + qy], twice[2 * lx + qx]
            plane[ly, lx, qy, qx, :, :, 0] = np.einsum("ab,cd->bdac", first, second)
            plane[ly, lx, qy, qx, :, :, 1] = np.einsum("ab,cd->bdac", side[own // 2] @ first, side[own % 2] @ second)
        planes.append(halved(plane.reshape(1024, 128)))
    t["zmaps"] = np.stack(zmaps)
    t["planes"] = np.stack(planes)
    spread = np.zeros((96, 128))
    for rank in range(96):
        spread[rank, rank // 6 * 8 + rank % 6] = 1
    t["spread"] = spread
    gather = np.zeros((2, 2, 4, 16, 128))
    shift = np.zeros((3, 8, 16, 8, 16))
    lanes = np.zeros((2, 3, 128, 256))
    for pz in range(2):
        for py in range(4):
            for px in range(16):
                source = (py // 2) * 8 + px // 2
                gather[0, pz, py, px, source * 8 + pz * 4 + (py % 2) * 2 + px % 2] = 1
                if py in (0, 3) and px < 8:
                    gather[1, pz, py, px, ((py == 3) * 8 + px) * 8] = 1
    for wx in range(3):
        for px in range(16):
            if 0 <= px + wx - 1 < 16:
                for block in range(8):
                    shift[wx, block, px, block, px + wx - 1] = 1
        for phase in range(8):
            for r in range(8):
                place = phase // 2 * 64 + r * 8 + 1 + 2 * wx + phase % 2
                lanes[0, wx, phase * 8 + r, place] = 1
                lanes[1, wx, 64 + phase * 8 + r, place] = 1
    t["gather"] = np.concatenate([gather.reshape(256, 128), shift.reshape(384, 128)])
    t["lanes"] = lanes.reshape(2, 384, 256)
    sel_three = np.zeros((256, 512))
    for gy in range(2):
        for px in range(4):
            for node in range(1, 7):
                gx = 2 * px - 3 + node
                if 0 <= gx < 8:
                    for r in range(8):
                        sel_three[gy * 128 + 64 + gx * 8 + r, px * 128 + gy * 64 + r * 8 + node] = 1
    t["sel_three"] = sel_three
    sel_two = np.zeros((128, 512))
    for px in range(2):
        for fy in range(2):
            for node in range(1, 7):
                bx = 2 * px - 3 + node
                if 0 <= bx < 4:
                    for r in range(8):
                        sel_two[64 + bx * 8 + r, (px * 2 + fy) * 128 + fy * 64 + r * 8 + node] = 1
    t["sel_two"] = sel_two
    back = np.zeros((16, 16, 256))
    for source in range(16):
        for lp in range(8):
            lz, ly, lx = octant(lp)
            row = lz * 64 + ((source // 8) * 2 + ly) * 16 + (source % 8) * 2 + lx
            back[source, lp, row] = 1
            back[source, 8 + lp, 128 + row] = 1
    t["back"] = back.reshape(256, 256)
    choose = np.zeros((49, 8, 316))
    number = 0
    for cell in range(49):
        for x in range(7):
            if max(abs(cell // 7 - 3), abs(cell % 7 - 3), abs(x - 3)) > 1:
                choose[cell, x, number] = 1
                number += 1
    t["choose"] = choose.reshape(392, 316)
    return t


def top_rows(levels_z):
    table = np.zeros((levels_z // 2, 4, 9, 2, 8, 256))
    for half in range(levels_z // 2):
        for k in range(4):
            for block in range(9):
                for fz in range(2):
                    z = 2 * (half + block // 3 - 1) + fz
                    y = k + block % 3 - 1
                    if 0 <= z < levels_z and 0 <= y < 4:
                        for px in range(4):
                            table[half, k, block, fz, px, px * 32 + z * 4 + y] = 1
                    z = 2 * (half // 2 + block // 3 - 1) + fz
                    for fy in range(2):
                        y = 2 * (k // 2 + block % 3 - 1) + fy
                        if 0 <= z < levels_z // 2 and 0 <= y < 4:
                            for px in range(2):
                                table[half, k, block, fz, 4 + px, 128 + (px * 2 + fy) * 16 + z * 4 + y] = 1
    return table.reshape(levels_z // 2 * 4, 144, 256)[:, :, :192]


def back_tops():
    table = np.zeros((4, 2, 16, 16, 8, TOPS))
    for gz in range(4):
        for k in range(2):
            for source in range(16):
                gy, gx = source // 8, source % 8
                for q in range(8):
                    table[gz, k, source, q, q, gy * 16 + gx] = 1
                table[gz, k, source, 8, gz % 2 * 4 + gy * 2 + gx % 2, 32 + gx // 2] = 1
                table[gz, k, source, 9, gz // 2 * 4 + k * 2 + gx // 2 % 2, 36 + gx // 4] = 1
    return table.reshape(8, 256, 8 * TOPS)


def split(value):
    if isinstance(value, tuple):
        return value
    high = value.astype(BF16)
    return high, (value - high.astype(F32)).astype(BF16)


def fdot(a, b, turned=False):
    (a_high, a_low), (b_high, b_low) = split(a), split(b)
    return bdot(a_high, b_high, turned) + (bdot(a_high, b_low, turned) + bdot(a_low, b_high, turned))


def bdot(a, b, turned=False):
    return lax.dot_general(a, b, (((1,), (1 if turned else 0,)), ((), ())), preferred_element_type=F32)


def rows_to_lanes(value, count):
    rows = value.shape[0] // count
    return jnp.concatenate([value[rows * n : rows * n + rows] for n in range(count)], axis=1)


def lanes_to_rows(value, count):
    width = value.shape[1] // count
    return jnp.concatenate([value[:, width * n : width * n + width] for n in range(count)], axis=0)


def upward(leaves, spread, c):
    order = c("leaf_order")[0]
    parts = [bdot(order, part) for part in split(leaves)]
    mixed = []
    for part in parts:
        lines = []
        for node in range(8):
            lines.append(
                jnp.concatenate([part[16 * n : 16 * n + 16, 64 * node : 64 * node + 64] for n in range(4)], axis=1)
            )
        mixed.append(jnp.concatenate(lines, axis=0).astype(BF16))
    mixed = fdot(c("up"), tuple(mixed))
    four = fdot(mixed[:64], c("pair_up"))
    upper = jnp.concatenate([rows_to_lanes(mixed[64:96], 4), rows_to_lanes(mixed[96:], 4)], axis=0)
    upper = fdot(upper, c("planes"))
    three, two = upper[:8, :64], upper[8:, 64:]
    rest = jnp.concatenate(
        [rows_to_lanes(four, 8), rows_to_lanes(three, 8), rows_to_lanes(two, 8), jnp.zeros((6, 512), F32)], axis=0
    )
    every = [jnp.concatenate([part.astype(BF16), extra], axis=0) for part, extra in zip(parts, split(rest))]
    return fdot(tuple(every), spread, turned=True)


def spread_ranks(turned_compress, c):
    return tuple(bdot(c("spread")[0], part).astype(BF16) for part in split(turned_compress))


def messages(packed, roll):
    tiles = []
    for q in range(8):
        first = q % 4 * 16 + q // 4 * 8
        tiles.append(packed[first : first + 8])
    for q in range(8):
        lines = [packed[64 + q : 65 + q]] + ([packed[72:73], packed[73:74]] if q == 0 else [])
        tiles.append(jnp.concatenate(lines + [jnp.zeros((8 - len(lines), 128), F32)], axis=0))
    lane = lax.broadcasted_iota(jnp.int32, (8, 128), 1)
    for bit in (1, 2, 4, 8):
        upper = lane // 8 // bit % 2 == 1
        for n in range(16):
            if n & bit == 0:
                low, high = tiles[n], tiles[n | bit]
                tiles[n] = jnp.where(upper, roll(high, 8 * bit, 1), low)
                tiles[n | bit] = jnp.where(upper, high, roll(low, 128 - 8 * bit, 1))
    return tiles


def top_row(tiles, roll):
    lane = lax.broadcasted_iota(jnp.int32, (8, 128), 1)
    mask = lane // 8 == 8
    sums = [jnp.zeros((8, 128), F32) for _ in range(3)]
    for n in range(16):
        kept = jnp.where(mask, tiles[n], 0.0)
        gx = n % 8
        sums[n // 8] += roll(kept, 8 * gx, 1) if gx else kept
        sums[2] += roll(kept, 8 * (gx // 2), 1) if gx // 2 else kept
    return jnp.concatenate([sums[0][1:2], sums[1][1:2], sums[2][2:3]], axis=1)


def assemble(received, c):
    picked = bdot(c("gather"), received.astype(BF16))
    lane = lax.broadcasted_iota(jnp.int32, (128, 128), 1)
    return jnp.where(lane < 64, picked[:128], picked[128:]).astype(BF16)


def widen(raw, blocks, five, four, c):
    narrow = jnp.concatenate([raw[z, y] for z, y in blocks], axis=0)
    wide, fours = [], []
    for start in range(0, len(blocks), 8):
        shifted = bdot(c("shift"), narrow[16 * start : 16 * start + 128]).astype(BF16)
        wide.append(rows_to_lanes(shifted, 3))
    wide = jnp.concatenate(wide, axis=0)
    result = bdot(wide, c("lanes_five")).astype(BF16)
    for n, (z, y) in enumerate(blocks):
        five[z, y] = result[16 * n : 16 * n + 16]
        if z in (0, 1, 3) and y in (0, 1, 4, 5):
            fours.append((n, (0, 1, 3).index(z), (0, 1, 4, 5).index(y)))
    result = bdot(jnp.concatenate([wide[16 * n : 16 * n + 16] for n, _, _ in fours], axis=0), c("lanes_four"))
    for place, (_, z, y) in enumerate(fours):
        four[z, y] = result[16 * place : 16 * place + 16].astype(BF16)


OWN = [(z, y) for z in (1, 2) for y in range(1, 5)]
AROUND = [(z, y) for z in range(4) for y in range(6) if (z, y) not in OWN]


def top_blocks(rows, pick, c):
    three = jnp.concatenate([row[:, :256] for row in rows], axis=0).astype(BF16)
    pairs = []
    for n in range(16):
        first = n // 4 * 8 + n % 4
        pairs.append(rows[first][:, 256:] + rows[first + 4][:, 256:])
    two = jnp.concatenate(pairs, axis=0).astype(BF16)
    stacked = jnp.concatenate(
        [
            lanes_to_rows(bdot(three, c("sel_three")), 4),
            lanes_to_rows(bdot(two, c("sel_two")), 4),
        ],
        axis=0,
    ).astype(BF16)
    return bdot(pick, stacked)


def lift_up(summed):
    total = summed[0].astype(F32)
    for n in range(1, 16):
        total = total + summed[n].astype(F32)
    return total


def down_top(summed, expand, c):
    row = lax.broadcasted_iota(jnp.int32, (16, 128), 0)
    scale = jnp.where(row < 8, 0.5, jnp.where(row == 8, 0.25, 0.125))
    fields = fdot((summed * scale)[:, :96], expand)
    two, three = lanes_to_rows(fields[9:10], 8), lanes_to_rows(fields[8:9], 8)
    zero = jnp.zeros((8, 64), F32)
    upper = jnp.concatenate(
        [jnp.concatenate([three, zero], axis=1), jnp.concatenate([zero, two], axis=1)], axis=0
    )
    upper = fdot(upper, c("planes"), turned=True)
    four = fdot(lanes_to_rows(fields[:8], 8), c("pair_up"), turned=True)
    five = fdot(
        c("down"),
        jnp.concatenate([four, lanes_to_rows(upper[:8], 4), lanes_to_rows(upper[8:], 4)], axis=0),
    )
    results = []
    for q in range(8):
        part = five[q // 4 * 64 : q // 4 * 64 + 64, q % 4 * 64 : q % 4 * 64 + 64]
        results.append(rows_to_lanes(part, 8))
    return jnp.concatenate(results, axis=0)


def expand_five(summed, expand):
    parts = []
    for q in range(8):
        pz, lane = q // 4, 128 * (q % 4)
        parts.append(summed[8 * pz : 8 * pz + 8, lane : lane + 128])
    return fdot(jnp.concatenate(parts, axis=0)[:, :96], expand)


def down_five(result, lines, out_ref):
    for q in range(8):
        qz, qy, qx = octant(q)
        for lz in range(2):
            for ly in range(2):
                first = lz * 32 + qz * 16 + ly * 8 + qy * 4 + qx
                source = q * 8 + lz * 4 + ly * 2
                for n in range(4):
                    lines[n, pl.ds(first, 2, stride=2), :] = result[source : source + 2, 128 * n : 128 * n + 128]
    for n in range(4):
        out_ref[:, 128 * n : 128 * n + 128] = lines[n]


PAIRS = {"leaf_order": (64, 64), "spread": (128, 96), "pair_up": (256, 64)}
NARROW = {"lanes_five": 384, "lanes_four": 384, "back": 256}
SELECT = {"sel_three": 256, "sel_two": 128}


def places(sizes):
    start, found = 0, {}
    for name, rows in sizes.items():
        found[name] = start, rows
        start += -(-rows // 16) * 16
    return found, start


PAIR_PLACES, PAIR_ROWS = places({name: shape[0] for name, shape in PAIRS.items()})
NARROW_PLACES, NARROW_ROWS = places(NARROW)
SELECT_PLACES, SELECT_ROWS = places(SELECT)


def halved(value):
    value = value.astype(np.float32)
    high = value.astype(jnp.bfloat16)
    return np.stack([high, (value - high.astype(np.float32)).astype(jnp.bfloat16)])


def packed_tables(groups):
    t = tables()
    t["lanes_five"], t["lanes_four"] = t["lanes"]
    t["spread"] = t["spread"].T
    pairs = np.zeros((PAIR_ROWS, 128))
    for name, (start, rows) in PAIR_PLACES.items():
        pairs[start : start + rows, : PAIRS[name][1]] = t[name]
    narrow = np.zeros((NARROW_ROWS, 256))
    for name, (start, rows) in NARROW_PLACES.items():
        narrow[start : start + rows] = t[name]
    select = np.zeros((SELECT_ROWS, 512))
    for name, (start, rows) in SELECT_PLACES.items():
        select[start : start + rows] = t[name]
    short = lambda value: value.astype(jnp.bfloat16)
    return [
        halved(pairs), short(t["choose"]), short(t["gather"]), short(narrow), short(select),
        t["zmaps"], t["planes"], short(top_rows(groups // 4)), short(back_tops()),
    ]


def getter(pairs, gather, narrow, select, zmaps, planes):
    def get(name):
        if name in ("up", "down"):
            start = 0 if name == "up" else 2
            return zmaps[start], zmaps[start + 1]
        if name == "planes":
            return planes[0], planes[1]
        if name == "gather":
            return gather[0:256]
        if name == "shift":
            return gather[256:640]
        if name in PAIRS:
            start, rows = PAIR_PLACES[name]
            lanes = PAIRS[name][1]
            return tuple(pairs[half, start : start + rows, 0:lanes] for half in range(2))
        if name in NARROW:
            start, rows = NARROW_PLACES[name]
            return narrow[start : start + rows]
        start, rows = SELECT_PLACES[name]
        return select[start : start + rows]

    return get


def place_transfers(m2l, choose, weights, roll):
    for rank in range(0, 8, 2):
        if rank == 6:
            weights[:, 48:64, :] = jnp.zeros((49, 16, 256), BF16)
            continue
        sides = [[], []]
        for n in (rank, rank + 1):
            rows = jnp.concatenate([m2l[n], jnp.zeros((32, 316), BF16)], axis=0)
            low = bdot(choose[0:280, 0:256], rows[:, 0:256], turned=True)
            high = bdot(choose[280:392, 128:316], rows[:, 128:316], turned=True)
            value = jnp.concatenate([low, high], axis=0)
            sides[0].append(value.reshape(49, 8, 128))
            sides[1].append(roll(value, 1, 0).reshape(49, 8, 128))
        for px in range(2):
            both = jnp.concatenate(sides[px], axis=1).astype(BF16)
            weights[:, 8 * rank : 8 * rank + 16, 128 * px : 128 * px + 128] = both


def block_transfers(weights, pz, py, block):
    wz, wy = block // 3, block % 3
    cells = [(2 * wz + fz + 1 - pz) * 7 + 2 * wy + fy + 1 - py for fz in range(2) for fy in range(2)]
    return jnp.concatenate([weights[cell] for cell in cells], axis=0)


def far_tops(four, top_ref, weights, back_top):
    lefts = []
    for block in range(9):
        wz, wy = block // 3, block % 3
        fz_parts = [top_ref[16 * block + 8 * fz : 16 * block + 8 * fz + 8, :] for fz in range(2)]
        tops = jnp.concatenate([jnp.concatenate(fz_parts, axis=1), jnp.zeros((8, 256), F32)], axis=0)
        lefts.append(jnp.concatenate([four[wz, wy : wy + 2].reshape(32, 256), tops.astype(BF16)], axis=0))
    pieces = []
    for child in range(4):
        value = None
        for block in range(9):
            product = bdot(lefts[block], block_transfers(weights, child // 2, child % 2, block))
            value = product if value is None else value + product
        short = value.astype(BF16)
        pieces += [short[:, :128], short[:, 128:]]
    return bdot(back_top, jnp.concatenate(pieces, axis=0)).astype(BF16)


def far_five(five, weights, back, py):
    values = []
    for pz in range(2):
        value = None
        for block in range(9):
            wz, wy = block // 3, block % 3
            left = five[wz : wz + 2, wy : wy + 4].reshape(128, 256)
            product = bdot(left, block_transfers(weights, pz, py, block))
            value = product if value is None else value + product
        values.append(value.astype(BF16))
    return bdot(back, jnp.concatenate(values, axis=0)).astype(BF16)


DIRECTIONS = [(dz, dk) for dz in (-1, 0, 1) for dk in (-1, 0, 1) if (dz, dk) != (0, 0)]


def halo_ranges(step, size):
    if step == 0:
        return pl.ds(1, size), pl.ds(1, size)
    if step == 1:
        return pl.ds(size, 1), pl.ds(0, 1)
    return pl.ds(1, 1), pl.ds(size + 1, 1)


def kernel(groups, *refs):
    sources, out_ref, scratch = refs[:13], refs[13], refs[14:]
    (
        leaf, m2l, compress, expand, pairs, choose, gather, narrow, select, zmaps, planes, pick, back_top,
        weights, message, received, row_ref, raw, five, four, top_ref, reply_top, reply_five, answer_top, answer_five,
        lines, load, send_a, recv_a, send_t, recv_t, send_halo, recv_halo, send_d, recv_d,
    ) = scratch
    o, v = lax.axis_index("oct"), lax.axis_index("dev")
    gz, k, gy, gx = o // 4, o % 4, v // 8, v % 8
    roll = pltpu.roll
    c = getter(pairs, gather, narrow, select, zmaps, planes)

    loads = {}
    for n, target in enumerate(scratch[:13]):
        source = sources[n]
        if target is zmaps:
            source = source.at[gz % 2]
        if target is planes:
            source = source.at[gy % 2 * 2 + gx % 2]
        if target is pick:
            source = source.at[gz // 2 * 4 + k]
        if target is back_top:
            source = source.at[gz % 4 * 2 + k % 2]
        loads[n] = pltpu.make_async_copy(source, target, load.at[n])
    for n in (0, 4, 9, 10, 2):
        loads[n].start()

    raw[...] = jnp.zeros(raw.shape, BF16)
    barrier = pltpu.get_barrier_semaphore()
    layers = groups // 4
    partners = [(n, 0) for n in range(1, layers)] + [(0, n) for n in range(1, 4)]
    partners += [(dz % layers, dk % 4) for dz in (-1, 1) for dk in (-1, 1)]
    for dz, dk in partners:
        target = lax.rem(gz + dz, layers) * 4 + lax.rem(k + dk, 4)
        pl.semaphore_signal(barrier, inc=1, device_id=(target, v), device_id_type=MESH)
    for n in range(1, 16):
        pl.semaphore_signal(barrier, inc=1, device_id=(o, lax.rem(v + n, 16)), device_id_type=MESH)
    for n in (1, 5, 6, 7, 8, 11, 12, 3):
        loads[n].start()

    for n in (0, 4, 9, 10, 2):
        loads[n].wait()
    packed = upward(leaf[...], spread_ranks(compress[...], c), c)
    tiles = messages(packed, roll)
    for n in range(16):
        message[n] = tiles[n]
    received[v] = message[v]
    pl.semaphore_wait(barrier, 15 + len(partners))

    def across(source, target, sems, n):
        return pltpu.make_async_remote_copy(
            src_ref=source.at[lax.rem(v + n, 16)], dst_ref=target.at[v], send_sem=sems[0], recv_sem=sems[1],
            device_id=(o, lax.rem(v + n, 16)), device_id_type=MESH,
        )

    def along_k(n):
        return pltpu.make_async_remote_copy(
            src_ref=row_ref.at[pl.ds(o, 1)], dst_ref=row_ref.at[pl.ds(o, 1)],
            send_sem=send_t.at[0], recv_sem=recv_t.at[0],
            device_id=(gz * 4 + lax.rem(k + n, 4), v), device_id_type=MESH,
        )

    def along_z(n):
        return pltpu.make_async_remote_copy(
            src_ref=row_ref.at[pl.ds(gz * 4, 4)], dst_ref=row_ref.at[pl.ds(gz * 4, 4)],
            send_sem=send_t.at[1], recv_sem=recv_t.at[1],
            device_id=(lax.rem(gz + n, layers) * 4 + k, v), device_id_type=MESH,
        )

    def whole(source, target, count, sems):
        return pltpu.make_async_remote_copy(
            src_ref=source.at[pl.ds(0, count)], dst_ref=target.at[pl.ds(0, count)], send_sem=sems[0], recv_sem=sems[1],
            device_id=(o, lax.rem(v + 1, 16)), device_id_type=MESH,
        )

    sems_a = (send_a, recv_a)
    for n in range(1, 16):
        across(message, received, sems_a, n).start()
    for n in (1, 5, 6, 7, 8, 11, 12, 3):
        loads[n].wait()
    place_transfers(m2l, choose, weights, roll)
    whole(message, received, 15, sems_a).wait_recv()

    got = [received[n] for n in range(16)]
    row_ref[o] = top_row(got, roll)
    for n in range(1, 4):
        along_k(n).start()
    raw[1:3, 1:5] = assemble(jnp.concatenate(got, axis=0), c).reshape(2, 4, 16, 128)

    def halo(number, dz, dk, sign):
        from_z, to_z = halo_ranges(dz, 2)
        from_y, to_y = halo_ranges(dk, 4)
        return pltpu.make_async_remote_copy(
            src_ref=raw.at[from_z, from_y], dst_ref=raw.at[to_z, to_y],
            send_sem=send_halo.at[number], recv_sem=recv_halo.at[number],
            device_id=((gz + sign * dz) * 4 + k + sign * dk, v), device_id_type=MESH,
        )

    def inside(dz, dk):
        return (gz + dz >= 0) & (gz + dz < groups // 4) & (k + dk >= 0) & (k + dk < 4)

    for number, (dz, dk) in enumerate(DIRECTIONS):
        @pl.when(inside(dz, dk))
        def _():
            halo(number, dz, dk, 1).start()

    def rows_of(step):
        return whole(row_ref, row_ref, (3, groups - 4)[step], (send_t.at[step], recv_t.at[step]))

    rows_of(0).wait_recv()
    for n in range(1, layers):
        along_z(n).start()

    widen(raw, OWN, five, four, c)

    for number, (dz, dk) in enumerate(DIRECTIONS):
        @pl.when(inside(-dz, -dk))
        def _():
            halo(number, dz, dk, -1).wait_recv()

    widen(raw, AROUND, five, four, c)
    returned_five = (reply_five, answer_five, (send_d.at[0], recv_d.at[0]))
    returned_top = (reply_top, answer_top, (send_d.at[1], recv_d.at[1]))
    for py in range(2):
        part = far_five(five, weights, c("back"), py).reshape(16, 16, 256)
        reply_five[:, :, 256 * py : 256 * py + 256] = part
    answer_five[v] = reply_five[v]
    for n in range(1, 16):
        across(*returned_five, n).start()

    rows_of(1).wait_recv()
    rows = [row_ref[n] for n in range(groups)]
    top_ref[...] = top_blocks(rows, pick[...], c)
    reply_top[...] = far_tops(four, top_ref, weights, back_top[...]).reshape(16, 16, 128)
    answer_top[v] = reply_top[v]
    for n in range(1, 16):
        across(*returned_top, n).start()

    split_expand = split(expand[...])
    whole(*returned_five[:2], 15, returned_five[2]).wait_recv()
    low = expand_five(lift_up(answer_five), split_expand)
    whole(message, received, 15, sems_a).wait_send()
    for number, (dz, dk) in enumerate(DIRECTIONS):
        @pl.when(inside(dz, dk))
        def _():
            halo(number, dz, dk, 1).wait_send()

    whole(*returned_top[:2], 15, returned_top[2]).wait_recv()
    above = down_top(lift_up(answer_top), split_expand, c)
    down_five(low + above, lines, out_ref)
    for source, target, sems in (returned_five, returned_top):
        whole(source, target, 15, sems).wait_send()
    for step in range(2):
        rows_of(step).wait_send()


def on_device(groups, leaf_multipoles, m2l_ops, compress, expand):
    values = [leaf_multipoles, m2l_ops.transpose(1, 2, 0), compress.T, expand]
    values += [jnp.asarray(value) for value in packed_tables(groups)]
    dma = pltpu.SemaphoreType.DMA
    loaded = [pltpu.VMEM(value.shape, value.dtype) for value in values[:-4]]
    loaded += [pltpu.VMEM(value.shape[1:], value.dtype) for value in values[-4:]]
    return pl.pallas_call(
        lambda *refs: kernel(groups, *refs),
        out_shape=jax.ShapeDtypeStruct((64, 512), F32),
        in_specs=[pl.BlockSpec(memory_space=pltpu.HBM)] * len(values),
        out_specs=pl.BlockSpec(memory_space=pltpu.VMEM),
        scratch_shapes=loaded
        + [
            pltpu.VMEM((49, 64, 256), BF16),
            pltpu.VMEM((16, 8, 128), F32),
            pltpu.VMEM((16, 8, 128), F32),
            pltpu.VMEM((groups, 1, 384), F32),
            pltpu.VMEM((4, 6, 16, 128), BF16),
            pltpu.VMEM((4, 6, 16, 256), BF16),
            pltpu.VMEM((3, 4, 16, 256), BF16),
            pltpu.VMEM((144, 128), F32),
            pltpu.VMEM((16, 16, 128), BF16),
            pltpu.VMEM((16, 16, 512), BF16),
            pltpu.VMEM((16, 16, 128), BF16),
            pltpu.VMEM((16, 16, 512), BF16),
            pltpu.VMEM((4, 64, 128), F32),
            dma((13,)),
            dma, dma, dma((2,)), dma((2,)), dma((8,)), dma((8,)), dma((2,)), dma((2,)),
        ],
        compiler_params=pltpu.CompilerParams(
            collective_id=0, has_side_effects=True, vmem_limit_bytes=55000 * 1024
        ),
        cost_estimate=pl.CostEstimate(flops=1_000_000_000, bytes_accessed=6_000_000, transcendentals=0),
    )(*values)


def solution(mesh):
    groups = mesh.shape["oct"]
    placed = (P(("oct", "dev"), None), P(None, "dev", None), P(), P())
    return jax.shard_map(
        lambda *args: on_device(groups, *args),
        mesh=mesh, in_specs=placed, out_specs=P(("oct", "dev"), None), check_vma=False,
    )
```

```python
import math

import jax
import jax.numpy as jnp
import numpy as np
from jax import lax
from jax.experimental import pallas as pl
from jax.experimental.pallas import tpu as pltpu
from jax.sharding import PartitionSpec as P


F32 = jnp.float32
BF16 = jnp.bfloat16
MESH = pl.DeviceIdType.MESH
TOPS = 48


def side_maps():
    ids = np.arange(8, dtype=np.float64)
    angles = (2 * ids + 1) * math.pi / 16
    points = np.cos(angles)
    degrees = np.arange(1, 8, dtype=np.float64)
    parent = np.cos(angles[:, None] * degrees[None, :])
    maps = []
    for side in range(2):
        child = np.cos(np.arccos((points + 2 * side - 1) / 2)[:, None] * degrees[None, :])
        maps.append(1 / 8 + 2 / 8 * parent @ child.T)
    return np.stack(maps)


def octant(number):
    return number // 4, number // 2 % 2, number % 2


def tables():
    side = side_maps()
    t = {}
    leaf_order = np.zeros((64, 64))
    up_five = np.zeros((8, 8, 8, 2, 8))
    for box in range(64):
        a, b, c = box // 16, box // 4 % 4, box % 4
        parent = (a // 2) * 4 + (b // 2) * 2 + c // 2
        leaf_order[((b % 2) * 2 + c % 2) * 16 + (a % 2) * 8 + parent, box] = 1
        up_five[:, parent, :, a % 2, parent] = side[a % 2]
    t["leaf_order"] = leaf_order
    pair = np.zeros((2, 2, 8, 8, 8, 8))
    for qy in range(2):
        for qx in range(2):
            pair[qy, qx] = np.einsum("ab,cd->bdac", side[qy], side[qx])
    t["pair_up"] = pair.reshape(256, 64)
    twice = np.stack([side[a // 2] @ side[a % 2] for a in range(4)])
    zmaps, planes = [], []
    for own in range(2):
        upper = np.stack([twice, side[own] @ twice])
        up = np.zeros((2, 4, 8, 8, 2, 8))
        down = np.zeros((2, 8, 8, 128))
        for box in range(8):
            lz, rest = box // 4, box % 4
            for qz in range(2):
                for level in range(2):
                    up[level, rest, :, :, qz, box] = upper[level, 2 * lz + qz]
                    start = 64 + 32 * level + 8 * rest
                    down[qz, :, box, start : start + 8] = upper[level, 2 * lz + qz].T
                for node in range(8):
                    down[qz, :, box, node * 8 + box] = side[qz][node]
        up = np.concatenate([up_five.reshape(64, 128), up.reshape(64, 128)])
        zmaps.append(np.concatenate([halved(up), halved(down.reshape(128, 128))]))
    for own in range(4):
        plane = np.zeros((2, 2, 2, 2, 8, 8, 2, 8, 8))
        for ly, lx, qy, qx in np.ndindex(2, 2, 2, 2):
            first, second = twice[2 * ly + qy], twice[2 * lx + qx]
            plane[ly, lx, qy, qx, :, :, 0] = np.einsum("ab,cd->bdac", first, second)
            plane[ly, lx, qy, qx, :, :, 1] = np.einsum("ab,cd->bdac", side[own // 2] @ first, side[own % 2] @ second)
        planes.append(halved(plane.reshape(1024, 128)))
    t["zmaps"] = np.stack(zmaps)
    t["planes"] = np.stack(planes)
    spread = np.zeros((96, 128))
    for rank in range(96):
        spread[rank, rank // 6 * 8 + rank % 6] = 1
    t["spread"] = spread
    gather = np.zeros((2, 2, 4, 16, 128))
    shift = np.zeros((3, 8, 16, 8, 16))
    lanes = np.zeros((2, 3, 128, 256))
    for pz in range(2):
        for py in range(4):
            for px in range(16):
                source = (py // 2) * 8 + px // 2
                gather[0, pz, py, px, source * 8 + pz * 4 + (py % 2) * 2 + px % 2] = 1
                if py in (0, 3) and px < 8:
                    gather[1, pz, py, px, ((py == 3) * 8 + px) * 8] = 1
    for wx in range(3):
        for px in range(16):
            if 0 <= px + wx - 1 < 16:
                for block in range(8):
                    shift[wx, block, px, block, px + wx - 1] = 1
        for phase in range(8):
            for r in range(8):
                place = phase // 2 * 64 + r * 8 + 1 + 2 * wx + phase % 2
                lanes[0, wx, phase * 8 + r, place] = 1
                lanes[1, wx, 64 + phase * 8 + r, place] = 1
    t["gather"] = np.concatenate([gather.reshape(256, 128), shift.reshape(384, 128)])
    t["lanes"] = lanes.reshape(2, 384, 256)
    sel_three = np.zeros((256, 512))
    for gy in range(2):
        for px in range(4):
            for node in range(1, 7):
                gx = 2 * px - 3 + node
                if 0 <= gx < 8:
                    for r in range(8):
                        sel_three[gy * 128 + 64 + gx * 8 + r, px * 128 + gy * 64 + r * 8 + node] = 1
    t["sel_three"] = sel_three
    sel_two = np.zeros((128, 512))
    for px in range(2):
        for fy in range(2):
            for node in range(1, 7):
                bx = 2 * px - 3 + node
                if 0 <= bx < 4:
                    for r in range(8):
                        sel_two[64 + bx * 8 + r, (px * 2 + fy) * 128 + fy * 64 + r * 8 + node] = 1
    t["sel_two"] = sel_two
    back = np.zeros((16, 16, 256))
    for source in range(16):
        for lp in range(8):
            lz, ly, lx = octant(lp)
            row = lz * 64 + ((source // 8) * 2 + ly) * 16 + (source % 8) * 2 + lx
            back[source, lp, row] = 1
            back[source, 8 + lp, 128 + row] = 1
    t["back"] = back.reshape(256, 256)
    choose = np.zeros((49, 8, 316))
    number = 0
    for cell in range(49):
        for x in range(7):
            if max(abs(cell // 7 - 3), abs(cell % 7 - 3), abs(x - 3)) > 1:
                choose[cell, x, number] = 1
                number += 1
    t["choose"] = choose.reshape(392, 316)
    return t


def top_rows(levels_z):
    table = np.zeros((levels_z // 2, 4, 9, 2, 8, 256))
    for half in range(levels_z // 2):
        for k in range(4):
            for block in range(9):
                for fz in range(2):
                    z = 2 * (half + block // 3 - 1) + fz
                    y = k + block % 3 - 1
                    if 0 <= z < levels_z and 0 <= y < 4:
                        for px in range(4):
                            table[half, k, block, fz, px, px * 32 + z * 4 + y] = 1
                    z = 2 * (half // 2 + block // 3 - 1) + fz
                    for fy in range(2):
                        y = 2 * (k // 2 + block % 3 - 1) + fy
                        if 0 <= z < levels_z // 2 and 0 <= y < 4:
                            for px in range(2):
                                table[half, k, block, fz, 4 + px, 128 + (px * 2 + fy) * 16 + z * 4 + y] = 1
    return table.reshape(levels_z // 2 * 4, 144, 256)[:, :, :192]


def back_tops():
    table = np.zeros((4, 2, 16, 16, 8, TOPS))
    for gz in range(4):
        for k in range(2):
            for source in range(16):
                gy, gx = source // 8, source % 8
                for q in range(8):
                    table[gz, k, source, q, q, gy * 16 + gx] = 1
                table[gz, k, source, 8, gz % 2 * 4 + gy * 2 + gx % 2, 32 + gx // 2] = 1
                table[gz, k, source, 9, gz // 2 * 4 + k * 2 + gx // 2 % 2, 36 + gx // 4] = 1
    return table.reshape(8, 256, 8 * TOPS)


def split(value):
    if isinstance(value, tuple):
        return value
    high = value.astype(BF16)
    return high, (value - high.astype(F32)).astype(BF16)


def fdot(a, b, turned=False):
    (a_high, a_low), (b_high, b_low) = split(a), split(b)
    return bdot(a_high, b_high, turned) + (bdot(a_high, b_low, turned) + bdot(a_low, b_high, turned))


def bdot(a, b, turned=False):
    return lax.dot_general(a, b, (((1,), (1 if turned else 0,)), ((), ())), preferred_element_type=F32)


def rows_to_lanes(value, count):
    rows = value.shape[0] // count
    return jnp.concatenate([value[rows * n : rows * n + rows] for n in range(count)], axis=1)


def lanes_to_rows(value, count):
    width = value.shape[1] // count
    return jnp.concatenate([value[:, width * n : width * n + width] for n in range(count)], axis=0)


def upward(leaves, spread, c):
    order = c("leaf_order")[0]
    parts = [bdot(order, part) for part in split(leaves)]
    mixed = []
    for part in parts:
        lines = []
        for node in range(8):
            lines.append(
                jnp.concatenate([part[16 * n : 16 * n + 16, 64 * node : 64 * node + 64] for n in range(4)], axis=1)
            )
        mixed.append(jnp.concatenate(lines, axis=0).astype(BF16))
    mixed = fdot(c("up"), tuple(mixed))
    four = fdot(mixed[:64], c("pair_up"))
    upper = jnp.concatenate([rows_to_lanes(mixed[64:96], 4), rows_to_lanes(mixed[96:], 4)], axis=0)
    upper = fdot(upper, c("planes"))
    three, two = upper[:8, :64], upper[8:, 64:]
    rest = jnp.concatenate(
        [rows_to_lanes(four, 8), rows_to_lanes(three, 8), rows_to_lanes(two, 8), jnp.zeros((6, 512), F32)], axis=0
    )
    every = [jnp.concatenate([part.astype(BF16), extra], axis=0) for part, extra in zip(parts, split(rest))]
    return fdot(tuple(every), spread, turned=True)


def spread_ranks(turned_compress, c):
    return tuple(bdot(c("spread")[0], part).astype(BF16) for part in split(turned_compress))


def messages(packed, roll):
    tiles = []
    for q in range(8):
        first = q % 4 * 16 + q // 4 * 8
        tiles.append(packed[first : first + 8])
    for q in range(8):
        lines = [packed[64 + q : 65 + q]] + ([packed[72:73], packed[73:74]] if q == 0 else [])
        tiles.append(jnp.concatenate(lines + [jnp.zeros((8 - len(lines), 128), F32)], axis=0))
    lane = lax.broadcasted_iota(jnp.int32, (8, 128), 1)
    for bit in (1, 2, 4, 8):
        upper = lane // 8 // bit % 2 == 1
        for n in range(16):
            if n & bit == 0:
                low, high = tiles[n], tiles[n | bit]
                tiles[n] = jnp.where(upper, roll(high, 8 * bit, 1), low)
                tiles[n | bit] = jnp.where(upper, high, roll(low, 128 - 8 * bit, 1))
    return tiles


def top_row(tiles, roll):
    lane = lax.broadcasted_iota(jnp.int32, (8, 128), 1)
    mask = lane // 8 == 8
    sums = [jnp.zeros((8, 128), F32) for _ in range(3)]
    for n in range(16):
        kept = jnp.where(mask, tiles[n], 0.0)
        gx = n % 8
        sums[n // 8] += roll(kept, 8 * gx, 1) if gx else kept
        sums[2] += roll(kept, 8 * (gx // 2), 1) if gx // 2 else kept
    return jnp.concatenate([sums[0][1:2], sums[1][1:2], sums[2][2:3]], axis=1)


def assemble(received, c):
    picked = bdot(c("gather"), received.astype(BF16))
    lane = lax.broadcasted_iota(jnp.int32, (128, 128), 1)
    return jnp.where(lane < 64, picked[:128], picked[128:]).astype(BF16)


def widen(raw, blocks, five, four, c):
    narrow = jnp.concatenate([raw[z, y] for z, y in blocks], axis=0)
    wide, fours = [], []
    for start in range(0, len(blocks), 8):
        shifted = bdot(c("shift"), narrow[16 * start : 16 * start + 128]).astype(BF16)
        wide.append(rows_to_lanes(shifted, 3))
    wide = jnp.concatenate(wide, axis=0)
    result = bdot(wide, c("lanes_five")).astype(BF16)
    for n, (z, y) in enumerate(blocks):
        five[z, y] = result[16 * n : 16 * n + 16]
        if z in (0, 1, 3) and y in (0, 1, 4, 5):
            fours.append((n, (0, 1, 3).index(z), (0, 1, 4, 5).index(y)))
    result = bdot(jnp.concatenate([wide[16 * n : 16 * n + 16] for n, _, _ in fours], axis=0), c("lanes_four"))
    for place, (_, z, y) in enumerate(fours):
        four[z, y] = result[16 * place : 16 * place + 16].astype(BF16)


OWN = [(z, y) for z in (1, 2) for y in range(1, 5)]
AROUND = [(z, y) for z in range(4) for y in range(6) if (z, y) not in OWN]


def top_blocks(rows, pick, c):
    three = jnp.concatenate([row[:, :256] for row in rows], axis=0).astype(BF16)
    pairs = []
    for n in range(16):
        first = n // 4 * 8 + n % 4
        pairs.append(rows[first][:, 256:] + rows[first + 4][:, 256:])
    two = jnp.concatenate(pairs, axis=0).astype(BF16)
    stacked = jnp.concatenate(
        [
            lanes_to_rows(bdot(three, c("sel_three")), 4),
            lanes_to_rows(bdot(two, c("sel_two")), 4),
        ],
        axis=0,
    ).astype(BF16)
    return bdot(pick, stacked)


def lift_up(summed):
    total = summed[0].astype(F32)
    for n in range(1, 16):
        total = total + summed[n].astype(F32)
    return total


def down_top(summed, expand, c):
    row = lax.broadcasted_iota(jnp.int32, (16, 128), 0)
    scale = jnp.where(row < 8, 0.5, jnp.where(row == 8, 0.25, 0.125))
    fields = fdot((summed * scale)[:, :96], expand)
    two, three = lanes_to_rows(fields[9:10], 8), lanes_to_rows(fields[8:9], 8)
    zero = jnp.zeros((8, 64), F32)
    upper = jnp.concatenate(
        [jnp.concatenate([three, zero], axis=1), jnp.concatenate([zero, two], axis=1)], axis=0
    )
    upper = fdot(upper, c("planes"), turned=True)
    four = fdot(lanes_to_rows(fields[:8], 8), c("pair_up"), turned=True)
    five = fdot(
        c("down"),
        jnp.concatenate([four, lanes_to_rows(upper[:8], 4), lanes_to_rows(upper[8:], 4)], axis=0),
    )
    results = []
    for q in range(8):
        part = five[q // 4 * 64 : q // 4 * 64 + 64, q % 4 * 64 : q % 4 * 64 + 64]
        results.append(rows_to_lanes(part, 8))
    return jnp.concatenate(results, axis=0)


def expand_five(summed, expand):
    parts = []
    for q in range(8):
        pz, lane = q // 4, 128 * (q % 4)
        parts.append(summed[8 * pz : 8 * pz + 8, lane : lane + 128])
    return fdot(jnp.concatenate(parts, axis=0)[:, :96], expand)


def down_five(result, lines, out_ref):
    for q in range(8):
        qz, qy, qx = octant(q)
        for lz in range(2):
            for ly in range(2):
                first = lz * 32 + qz * 16 + ly * 8 + qy * 4 + qx
                source = q * 8 + lz * 4 + ly * 2
                for n in range(4):
                    lines[n, pl.ds(first, 2, stride=2), :] = result[source : source + 2, 128 * n : 128 * n + 128]
    for n in range(4):
        out_ref[:, 128 * n : 128 * n + 128] = lines[n]


PAIRS = {"leaf_order": (64, 64), "spread": (128, 96), "pair_up": (256, 64)}
NARROW = {"lanes_five": 384, "lanes_four": 384, "back": 256}
SELECT = {"sel_three": 256, "sel_two": 128}


def places(sizes):
    start, found = 0, {}
    for name, rows in sizes.items():
        found[name] = start, rows
        start += -(-rows // 16) * 16
    return found, start


PAIR_PLACES, PAIR_ROWS = places({name: shape[0] for name, shape in PAIRS.items()})
NARROW_PLACES, NARROW_ROWS = places(NARROW)
SELECT_PLACES, SELECT_ROWS = places(SELECT)


def halved(value):
    value = value.astype(np.float32)
    high = value.astype(jnp.bfloat16)
    return np.stack([high, (value - high.astype(np.float32)).astype(jnp.bfloat16)])


def packed_tables(groups):
    t = tables()
    t["lanes_five"], t["lanes_four"] = t["lanes"]
    t["spread"] = t["spread"].T
    pairs = np.zeros((PAIR_ROWS, 128))
    for name, (start, rows) in PAIR_PLACES.items():
        pairs[start : start + rows, : PAIRS[name][1]] = t[name]
    narrow = np.zeros((NARROW_ROWS, 256))
    for name, (start, rows) in NARROW_PLACES.items():
        narrow[start : start + rows] = t[name]
    select = np.zeros((SELECT_ROWS, 512))
    for name, (start, rows) in SELECT_PLACES.items():
        select[start : start + rows] = t[name]
    short = lambda value: value.astype(jnp.bfloat16)
    return [
        halved(pairs), short(t["choose"]), short(t["gather"]), short(narrow), short(select),
        t["zmaps"], t["planes"], short(top_rows(groups // 4)), short(back_tops()),
    ]


def getter(pairs, gather, narrow, select, zmaps, planes):
    def get(name):
        if name in ("up", "down"):
            start = 0 if name == "up" else 2
            return zmaps[start], zmaps[start + 1]
        if name == "planes":
            return planes[0], planes[1]
        if name == "gather":
            return gather[0:256]
        if name == "shift":
            return gather[256:640]
        if name in PAIRS:
            start, rows = PAIR_PLACES[name]
            lanes = PAIRS[name][1]
            return tuple(pairs[half, start : start + rows, 0:lanes] for half in range(2))
        if name in NARROW:
            start, rows = NARROW_PLACES[name]
            return narrow[start : start + rows]
        start, rows = SELECT_PLACES[name]
        return select[start : start + rows]

    return get


def place_transfers(m2l, choose, weights, roll):
    for rank in range(0, 8, 2):
        if rank == 6:
            weights[:, 48:64, :] = jnp.zeros((49, 16, 256), BF16)
            continue
        sides = [[], []]
        for n in (rank, rank + 1):
            rows = jnp.concatenate([m2l[n], jnp.zeros((32, 316), BF16)], axis=0)
            low = bdot(choose[0:280, 0:256], rows[:, 0:256], turned=True)
            high = bdot(choose[280:392, 128:316], rows[:, 128:316], turned=True)
            value = jnp.concatenate([low, high], axis=0)
            sides[0].append(value.reshape(49, 8, 128))
            sides[1].append(roll(value, 1, 0).reshape(49, 8, 128))
        for px in range(2):
            both = jnp.concatenate(sides[px], axis=1).astype(BF16)
            weights[:, 8 * rank : 8 * rank + 16, 128 * px : 128 * px + 128] = both


def block_transfers(weights, pz, py, block):
    wz, wy = block // 3, block % 3
    cells = [(2 * wz + fz + 1 - pz) * 7 + 2 * wy + fy + 1 - py for fz in range(2) for fy in range(2)]
    return jnp.concatenate([weights[cell] for cell in cells], axis=0)


def far_tops(four, top_ref, weights, back_top):
    lefts = []
    for block in range(9):
        wz, wy = block // 3, block % 3
        fz_parts = [top_ref[16 * block + 8 * fz : 16 * block + 8 * fz + 8, :] for fz in range(2)]
        tops = jnp.concatenate([jnp.concatenate(fz_parts, axis=1), jnp.zeros((8, 256), F32)], axis=0)
        lefts.append(jnp.concatenate([four[wz, wy : wy + 2].reshape(32, 256), tops.astype(BF16)], axis=0))
    pieces = []
    for child in range(4):
        value = None
        for block in range(9):
            product = bdot(lefts[block], block_transfers(weights, child // 2, child % 2, block))
            value = product if value is None else value + product
        short = value.astype(BF16)
        pieces += [short[:, :128], short[:, 128:]]
    return bdot(back_top, jnp.concatenate(pieces, axis=0)).astype(BF16)


def far_five(five, weights, back, py):
    values = []
    for pz in range(2):
        value = None
        for block in range(9):
            wz, wy = block // 3, block % 3
            left = five[wz : wz + 2, wy : wy + 4].reshape(128, 256)
            product = bdot(left, block_transfers(weights, pz, py, block))
            value = product if value is None else value + product
        values.append(value.astype(BF16))
    return bdot(back, jnp.concatenate(values, axis=0)).astype(BF16)


DIRECTIONS = [(dz, dk) for dz in (-1, 0, 1) for dk in (-1, 0, 1) if (dz, dk) != (0, 0)]


def halo_ranges(step, size):
    if step == 0:
        return pl.ds(1, size), pl.ds(1, size)
    if step == 1:
        return pl.ds(size, 1), pl.ds(0, 1)
    return pl.ds(1, 1), pl.ds(size + 1, 1)


def kernel(groups, *refs):
    sources, out_ref, scratch = refs[:13], refs[13], refs[14:]
    (
        leaf, m2l, compress, expand, pairs, choose, gather, narrow, select, zmaps, planes, pick, back_top,
        weights, message, received, row_ref, raw, five, four, top_ref, reply_top, reply_five, answer_top, answer_five,
        lines, load, send_a, recv_a, send_t, recv_t, send_halo, recv_halo, send_d, recv_d,
    ) = scratch
    o, v = lax.axis_index("oct"), lax.axis_index("dev")
    gz, k, gy, gx = o // 4, o % 4, v // 8, v % 8
    roll = pltpu.roll
    c = getter(pairs, gather, narrow, select, zmaps, planes)

    loads = {}
    for n, target in enumerate(scratch[:13]):
        source = sources[n]
        if target is zmaps:
            source = source.at[gz % 2]
        if target is planes:
            source = source.at[gy % 2 * 2 + gx % 2]
        if target is pick:
            source = source.at[gz // 2 * 4 + k]
        if target is back_top:
            source = source.at[gz % 4 * 2 + k % 2]
        loads[n] = pltpu.make_async_copy(source, target, load.at[n])
    for n in (0, 4, 9, 10, 2):
        loads[n].start()

    raw[...] = jnp.zeros(raw.shape, BF16)
    barrier = pltpu.get_barrier_semaphore()
    layers = groups // 4
    partners = [(n, 0) for n in sorted(range(1, layers), key=lambda n: abs(n - layers // 2))] + [(0, n) for n in range(1, 4)]
    partners += [(dz % layers, dk % 4) for dz in (-1, 1) for dk in (-1, 1)]
    for dz, dk in partners:
        target = lax.rem(gz + dz, layers) * 4 + lax.rem(k + dk, 4)
        pl.semaphore_signal(barrier, inc=1, device_id=(target, v), device_id_type=MESH)
    for n in range(1, 16):
        pl.semaphore_signal(barrier, inc=1, device_id=(o, lax.rem(v + n, 16)), device_id_type=MESH)
    for n in (1, 5, 6, 7, 8, 11, 12, 3):
        loads[n].start()

    for n in (0, 4, 9, 10, 2):
        loads[n].wait()
    packed = upward(leaf[...], spread_ranks(compress[...], c), c)
    tiles = messages(packed, roll)
    for n in range(16):
        message[n] = tiles[n]
    received[v] = message[v]
    pl.semaphore_wait(barrier, 15 + len(partners))

    def across(source, target, sems, n):
        return pltpu.make_async_remote_copy(
            src_ref=source.at[lax.rem(v + n, 16)], dst_ref=target.at[v], send_sem=sems[0], recv_sem=sems[1],
            device_id=(o, lax.rem(v + n, 16)), device_id_type=MESH,
        )

    def along_k(n):
        return pltpu.make_async_remote_copy(
            src_ref=row_ref.at[pl.ds(o, 1)], dst_ref=row_ref.at[pl.ds(o, 1)],
            send_sem=send_t.at[0], recv_sem=recv_t.at[0],
            device_id=(gz * 4 + lax.rem(k + n, 4), v), device_id_type=MESH,
        )

    def along_z(n):
        return pltpu.make_async_remote_copy(
            src_ref=row_ref.at[pl.ds(gz * 4, 4)], dst_ref=row_ref.at[pl.ds(gz * 4, 4)],
            send_sem=send_t.at[1], recv_sem=recv_t.at[1],
            device_id=(lax.rem(gz + n, layers) * 4 + k, v), device_id_type=MESH,
        )

    def whole(source, target, count, sems):
        return pltpu.make_async_remote_copy(
            src_ref=source.at[pl.ds(0, count)], dst_ref=target.at[pl.ds(0, count)], send_sem=sems[0], recv_sem=sems[1],
            device_id=(o, lax.rem(v + 1, 16)), device_id_type=MESH,
        )

    sems_a = (send_a, recv_a)
    for n in range(1, 16):
        across(message, received, sems_a, n).start()
    for n in (1, 5, 6, 7, 8, 11, 12, 3):
        loads[n].wait()
    place_transfers(m2l, choose, weights, roll)
    whole(message, received, 15, sems_a).wait_recv()

    got = [received[n] for n in range(16)]
    row_ref[o] = top_row(got, roll)
    for n in range(1, 4):
        along_k(n).start()
    raw[1:3, 1:5] = assemble(jnp.concatenate(got, axis=0), c).reshape(2, 4, 16, 128)

    def halo(number, dz, dk, sign):
        from_z, to_z = halo_ranges(dz, 2)
        from_y, to_y = halo_ranges(dk, 4)
        return pltpu.make_async_remote_copy(
            src_ref=raw.at[from_z, from_y], dst_ref=raw.at[to_z, to_y],
            send_sem=send_halo.at[number], recv_sem=recv_halo.at[number],
            device_id=((gz + sign * dz) * 4 + k + sign * dk, v), device_id_type=MESH,
        )

    def inside(dz, dk):
        return (gz + dz >= 0) & (gz + dz < groups // 4) & (k + dk >= 0) & (k + dk < 4)

    for number, (dz, dk) in enumerate(DIRECTIONS):
        @pl.when(inside(dz, dk))
        def _():
            halo(number, dz, dk, 1).start()

    def rows_of(step):
        return whole(row_ref, row_ref, (3, groups - 4)[step], (send_t.at[step], recv_t.at[step]))

    rows_of(0).wait_recv()
    for n in range(1, layers):
        along_z(n).start()

    widen(raw, OWN, five, four, c)

    for number, (dz, dk) in enumerate(DIRECTIONS):
        @pl.when(inside(-dz, -dk))
        def _():
            halo(number, dz, dk, -1).wait_recv()

    widen(raw, AROUND, five, four, c)
    returned = [(reply_five.at[n], answer_five.at[n], (send_d.at[n], recv_d.at[n])) for n in range(2)]
    returned_top = (reply_top, answer_top, (send_d.at[2], recv_d.at[2]))
    for py in range(2):
        reply_five[py] = far_five(five, weights, c("back"), py).reshape(16, 16, 256)
        answer_five[py, v] = reply_five[py, v]
        for n in range(1, 16):
            across(*returned[py], n).start()

    rows_of(1).wait_recv()
    rows = [row_ref[n] for n in range(groups)]
    top_ref[...] = top_blocks(rows, pick[...], c)
    reply_top[...] = far_tops(four, top_ref, weights, back_top[...]).reshape(16, 16, 128)
    answer_top[v] = reply_top[v]
    for n in range(1, 16):
        across(*returned_top, n).start()

    split_expand = split(expand[...])
    halves = []
    for py in range(2):
        whole(*returned[py][:2], 15, returned[py][2]).wait_recv()
        halves.append(lift_up(answer_five.at[py]))
    low = expand_five(jnp.concatenate(halves, axis=1), split_expand)
    whole(message, received, 15, sems_a).wait_send()
    for number, (dz, dk) in enumerate(DIRECTIONS):
        @pl.when(inside(dz, dk))
        def _():
            halo(number, dz, dk, 1).wait_send()

    whole(*returned_top[:2], 15, returned_top[2]).wait_recv()
    above = down_top(lift_up(answer_top), split_expand, c)
    down_five(low + above, lines, out_ref)
    for source, target, sems in (*returned, returned_top):
        whole(source, target, 15, sems).wait_send()
    for step in range(2):
        rows_of(step).wait_send()


def on_device(groups, leaf_multipoles, m2l_ops, compress, expand):
    values = [leaf_multipoles, m2l_ops.transpose(1, 2, 0), compress.T, expand]
    values += [jnp.asarray(value) for value in packed_tables(groups)]
    dma = pltpu.SemaphoreType.DMA
    loaded = [pltpu.VMEM(value.shape, value.dtype) for value in values[:-4]]
    loaded += [pltpu.VMEM(value.shape[1:], value.dtype) for value in values[-4:]]
    return pl.pallas_call(
        lambda *refs: kernel(groups, *refs),
        out_shape=jax.ShapeDtypeStruct((64, 512), F32),
        in_specs=[pl.BlockSpec(memory_space=pltpu.HBM)] * len(values),
        out_specs=pl.BlockSpec(memory_space=pltpu.VMEM),
        scratch_shapes=loaded
        + [
            pltpu.VMEM((49, 64, 256), BF16),
            pltpu.VMEM((16, 8, 128), F32),
            pltpu.VMEM((16, 8, 128), F32),
            pltpu.VMEM((groups, 1, 384), F32),
            pltpu.VMEM((4, 6, 16, 128), BF16),
            pltpu.VMEM((4, 6, 16, 256), BF16),
            pltpu.VMEM((3, 4, 16, 256), BF16),
            pltpu.VMEM((144, 128), F32),
            pltpu.VMEM((16, 16, 128), BF16),
            pltpu.VMEM((2, 16, 16, 256), BF16),
            pltpu.VMEM((16, 16, 128), BF16),
            pltpu.VMEM((2, 16, 16, 256), BF16),
            pltpu.VMEM((4, 64, 128), F32),
            dma((13,)),
            dma, dma, dma((2,)), dma((2,)), dma((8,)), dma((8,)), dma((3,)), dma((3,)),
        ],
        compiler_params=pltpu.CompilerParams(
            collective_id=0, has_side_effects=True, vmem_limit_bytes=55000 * 1024
        ),
        cost_estimate=pl.CostEstimate(flops=1_000_000_000, bytes_accessed=6_000_000, transcendentals=0),
    )(*values)


def solution(mesh):
    groups = mesh.shape["oct"]
    placed = (P(("oct", "dev"), None), P(None, "dev", None), P(), P())
    return jax.shard_map(
        lambda *args: on_device(groups, *args),
        mesh=mesh, in_specs=placed, out_specs=P(("oct", "dev"), None), check_vma=False,
    )
```

```python
import math

import jax
import jax.numpy as jnp
import numpy as np
from jax import lax
from jax.experimental import pallas as pl
from jax.experimental.pallas import tpu as pltpu
from jax.sharding import PartitionSpec as P


F32 = jnp.float32
BF16 = jnp.bfloat16
MESH = pl.DeviceIdType.MESH
TOPS = 48


def side_maps():
    ids = np.arange(8, dtype=np.float64)
    angles = (2 * ids + 1) * math.pi / 16
    points = np.cos(angles)
    degrees = np.arange(1, 8, dtype=np.float64)
    parent = np.cos(angles[:, None] * degrees[None, :])
    maps = []
    for side in range(2):
        child = np.cos(np.arccos((points + 2 * side - 1) / 2)[:, None] * degrees[None, :])
        maps.append(1 / 8 + 2 / 8 * parent @ child.T)
    return np.stack(maps)


def octant(number):
    return number // 4, number // 2 % 2, number % 2


def tables():
    side = side_maps()
    t = {}
    leaf_order = np.zeros((64, 64))
    up_five = np.zeros((8, 8, 8, 2, 8))
    for box in range(64):
        a, b, c = box // 16, box // 4 % 4, box % 4
        parent = (a // 2) * 4 + (b // 2) * 2 + c // 2
        leaf_order[((b % 2) * 2 + c % 2) * 16 + (a % 2) * 8 + parent, box] = 1
        up_five[:, parent, :, a % 2, parent] = side[a % 2]
    t["leaf_order"] = leaf_order
    pair = np.zeros((2, 2, 8, 8, 8, 8))
    for qy in range(2):
        for qx in range(2):
            pair[qy, qx] = np.einsum("ab,cd->bdac", side[qy], side[qx])
    t["pair_up"] = pair.reshape(256, 64)
    twice = np.stack([side[a // 2] @ side[a % 2] for a in range(4)])
    zmaps, planes = [], []
    for own in range(2):
        upper = np.stack([twice, side[own] @ twice])
        up = np.zeros((2, 4, 8, 8, 2, 8))
        down = np.zeros((2, 8, 8, 128))
        for box in range(8):
            lz, rest = box // 4, box % 4
            for qz in range(2):
                for level in range(2):
                    up[level, rest, :, :, qz, box] = upper[level, 2 * lz + qz]
                    start = 64 + 32 * level + 8 * rest
                    down[qz, :, box, start : start + 8] = upper[level, 2 * lz + qz].T
                for node in range(8):
                    down[qz, :, box, node * 8 + box] = side[qz][node]
        up = np.concatenate([up_five.reshape(64, 128), up.reshape(64, 128)])
        zmaps.append(np.concatenate([halved(up), halved(down.reshape(128, 128))]))
    for own in range(4):
        plane = np.zeros((2, 2, 2, 2, 8, 8, 2, 8, 8))
        for ly, lx, qy, qx in np.ndindex(2, 2, 2, 2):
            first, second = twice[2 * ly + qy], twice[2 * lx + qx]
            plane[ly, lx, qy, qx, :, :, 0] = np.einsum("ab,cd->bdac", first, second)
            plane[ly, lx, qy, qx, :, :, 1] = np.einsum("ab,cd->bdac", side[own // 2] @ first, side[own % 2] @ second)
        planes.append(halved(plane.reshape(1024, 128)))
    t["zmaps"] = np.stack(zmaps)
    t["planes"] = np.stack(planes)
    spread = np.zeros((96, 128))
    for rank in range(96):
        spread[rank, rank // 6 * 8 + rank % 6] = 1
    t["spread"] = spread
    gather = np.zeros((2, 2, 4, 16, 128))
    shift = np.zeros((3, 8, 16, 8, 16))
    lanes = np.zeros((2, 3, 128, 256))
    for pz in range(2):
        for py in range(4):
            for px in range(16):
                source = (py // 2) * 8 + px // 2
                gather[0, pz, py, px, source * 8 + pz * 4 + (py % 2) * 2 + px % 2] = 1
                if py in (0, 3) and px < 8:
                    gather[1, pz, py, px, ((py == 3) * 8 + px) * 8] = 1
    for wx in range(3):
        for px in range(16):
            if 0 <= px + wx - 1 < 16:
                for block in range(8):
                    shift[wx, block, px, block, px + wx - 1] = 1
        for phase in range(8):
            for r in range(8):
                place = phase // 2 * 64 + r * 8 + 1 + 2 * wx + phase % 2
                lanes[0, wx, phase * 8 + r, place] = 1
                lanes[1, wx, 64 + phase * 8 + r, place] = 1
    t["gather"] = np.concatenate([gather.reshape(256, 128), shift.reshape(384, 128)])
    t["lanes"] = lanes.reshape(2, 384, 256)
    sel_three = np.zeros((256, 512))
    for gy in range(2):
        for px in range(4):
            for node in range(1, 7):
                gx = 2 * px - 3 + node
                if 0 <= gx < 8:
                    for r in range(8):
                        sel_three[gy * 128 + 64 + gx * 8 + r, px * 128 + gy * 64 + r * 8 + node] = 1
    t["sel_three"] = sel_three
    sel_two = np.zeros((128, 512))
    for px in range(2):
        for fy in range(2):
            for node in range(1, 7):
                bx = 2 * px - 3 + node
                if 0 <= bx < 4:
                    for r in range(8):
                        sel_two[64 + bx * 8 + r, (px * 2 + fy) * 128 + fy * 64 + r * 8 + node] = 1
    t["sel_two"] = sel_two
    back = np.zeros((16, 16, 256))
    for source in range(16):
        for lp in range(8):
            lz, ly, lx = octant(lp)
            row = lz * 64 + ((source // 8) * 2 + ly) * 16 + (source % 8) * 2 + lx
            back[source, lp, row] = 1
            back[source, 8 + lp, 128 + row] = 1
    t["back"] = back.reshape(256, 256)
    choose = np.zeros((49, 8, 316))
    number = 0
    for cell in range(49):
        for x in range(7):
            if max(abs(cell // 7 - 3), abs(cell % 7 - 3), abs(x - 3)) > 1:
                choose[cell, x, number] = 1
                number += 1
    t["choose"] = choose.reshape(392, 316)
    return t


def top_rows(levels_z):
    table = np.zeros((levels_z // 2, 4, 9, 2, 8, 256))
    for half in range(levels_z // 2):
        for k in range(4):
            for block in range(9):
                for fz in range(2):
                    z = 2 * (half + block // 3 - 1) + fz
                    y = k + block % 3 - 1
                    if 0 <= z < levels_z and 0 <= y < 4:
                        for px in range(4):
                            table[half, k, block, fz, px, px * 32 + z * 4 + y] = 1
                    z = 2 * (half // 2 + block // 3 - 1) + fz
                    for fy in range(2):
                        y = 2 * (k // 2 + block % 3 - 1) + fy
                        if 0 <= z < levels_z // 2 and 0 <= y < 4:
                            for px in range(2):
                                table[half, k, block, fz, 4 + px, 128 + (px * 2 + fy) * 16 + z * 4 + y] = 1
    return table.reshape(levels_z // 2 * 4, 144, 256)[:, :, :192]


def back_tops():
    table = np.zeros((4, 2, 16, 16, 8, TOPS))
    for gz in range(4):
        for k in range(2):
            for source in range(16):
                gy, gx = source // 8, source % 8
                for q in range(8):
                    table[gz, k, source, q, q, gy * 16 + gx] = 1
                table[gz, k, source, 8, gz % 2 * 4 + gy * 2 + gx % 2, 32 + gx // 2] = 1
                table[gz, k, source, 9, gz // 2 * 4 + k * 2 + gx // 2 % 2, 36 + gx // 4] = 1
    return table.reshape(8, 256, 8 * TOPS)


def split(value):
    if isinstance(value, tuple):
        return value
    high = value.astype(BF16)
    return high, (value - high.astype(F32)).astype(BF16)


def fdot(a, b, turned=False):
    (a_high, a_low), (b_high, b_low) = split(a), split(b)
    return bdot(a_high, b_high, turned) + (bdot(a_high, b_low, turned) + bdot(a_low, b_high, turned))


def bdot(a, b, turned=False):
    return lax.dot_general(a, b, (((1,), (1 if turned else 0,)), ((), ())), preferred_element_type=F32)


def rows_to_lanes(value, count):
    rows = value.shape[0] // count
    return jnp.concatenate([value[rows * n : rows * n + rows] for n in range(count)], axis=1)


def lanes_to_rows(value, count):
    width = value.shape[1] // count
    return jnp.concatenate([value[:, width * n : width * n + width] for n in range(count)], axis=0)


def upward(leaves, spread, c):
    order = c("leaf_order")[0]
    parts = [bdot(order, part) for part in split(leaves)]
    mixed = []
    for part in parts:
        lines = []
        for node in range(8):
            lines.append(
                jnp.concatenate([part[16 * n : 16 * n + 16, 64 * node : 64 * node + 64] for n in range(4)], axis=1)
            )
        mixed.append(jnp.concatenate(lines, axis=0).astype(BF16))
    mixed = fdot(c("up"), tuple(mixed))
    four = fdot(mixed[:64], c("pair_up"))
    upper = jnp.concatenate([rows_to_lanes(mixed[64:96], 4), rows_to_lanes(mixed[96:], 4)], axis=0)
    upper = fdot(upper, c("planes"))
    three, two = upper[:8, :64], upper[8:, 64:]
    rest = jnp.concatenate(
        [rows_to_lanes(four, 8), rows_to_lanes(three, 8), rows_to_lanes(two, 8), jnp.zeros((6, 512), F32)], axis=0
    )
    every = [jnp.concatenate([part.astype(BF16), extra], axis=0) for part, extra in zip(parts, split(rest))]
    return fdot(tuple(every), spread, turned=True)


def spread_ranks(turned_compress, c):
    return tuple(bdot(c("spread")[0], part).astype(BF16) for part in split(turned_compress))


def messages(packed, roll):
    tiles = []
    for q in range(8):
        first = q % 4 * 16 + q // 4 * 8
        tiles.append(packed[first : first + 8])
    for q in range(8):
        lines = [packed[64 + q : 65 + q]] + ([packed[72:73], packed[73:74]] if q == 0 else [])
        tiles.append(jnp.concatenate(lines + [jnp.zeros((8 - len(lines), 128), F32)], axis=0))
    lane = lax.broadcasted_iota(jnp.int32, (8, 128), 1)
    for bit in (1, 2, 4, 8):
        upper = lane // 8 // bit % 2 == 1
        for n in range(16):
            if n & bit == 0:
                low, high = tiles[n], tiles[n | bit]
                tiles[n] = jnp.where(upper, roll(high, 8 * bit, 1), low)
                tiles[n | bit] = jnp.where(upper, high, roll(low, 128 - 8 * bit, 1))
    return tiles


def top_row(tiles, roll):
    lane = lax.broadcasted_iota(jnp.int32, (8, 128), 1)
    mask = lane // 8 == 8
    sums = [jnp.zeros((8, 128), F32) for _ in range(3)]
    for n in range(16):
        kept = jnp.where(mask, tiles[n], 0.0)
        gx = n % 8
        sums[n // 8] += roll(kept, 8 * gx, 1) if gx else kept
        sums[2] += roll(kept, 8 * (gx // 2), 1) if gx // 2 else kept
    return jnp.concatenate([sums[0][1:2], sums[1][1:2], sums[2][2:3]], axis=1)


def assemble(received, c):
    picked = bdot(c("gather"), received.astype(BF16))
    lane = lax.broadcasted_iota(jnp.int32, (128, 128), 1)
    return jnp.where(lane < 64, picked[:128], picked[128:]).astype(BF16)


def widen(raw, blocks, five, four, c):
    narrow = jnp.concatenate([raw[z, y] for z, y in blocks], axis=0)
    wide, fours = [], []
    for start in range(0, len(blocks), 8):
        shifted = bdot(c("shift"), narrow[16 * start : 16 * start + 128]).astype(BF16)
        wide.append(rows_to_lanes(shifted, 3))
    wide = jnp.concatenate(wide, axis=0)
    result = bdot(wide, c("lanes_five")).astype(BF16)
    for n, (z, y) in enumerate(blocks):
        five[z, y] = result[16 * n : 16 * n + 16]
        if z in (0, 1, 3) and y in (0, 1, 4, 5):
            fours.append((n, (0, 1, 3).index(z), (0, 1, 4, 5).index(y)))
    result = bdot(jnp.concatenate([wide[16 * n : 16 * n + 16] for n, _, _ in fours], axis=0), c("lanes_four"))
    for place, (_, z, y) in enumerate(fours):
        four[z, y] = result[16 * place : 16 * place + 16].astype(BF16)


OWN = [(z, y) for z in (1, 2) for y in range(1, 5)]
AROUND = [(z, y) for z in range(4) for y in range(6) if (z, y) not in OWN]


def top_blocks(rows, pick, c):
    three = jnp.concatenate([row[:, :256] for row in rows], axis=0).astype(BF16)
    pairs = []
    for n in range(16):
        first = n // 4 * 8 + n % 4
        pairs.append(rows[first][:, 256:] + rows[first + 4][:, 256:])
    two = jnp.concatenate(pairs, axis=0).astype(BF16)
    stacked = jnp.concatenate(
        [
            lanes_to_rows(bdot(three, c("sel_three")), 4),
            lanes_to_rows(bdot(two, c("sel_two")), 4),
        ],
        axis=0,
    ).astype(BF16)
    return bdot(pick, stacked)


def lift_up(summed):
    total = summed[0].astype(F32)
    for n in range(1, 16):
        total = total + summed[n].astype(F32)
    return total


def down_top(summed, expand, c):
    row = lax.broadcasted_iota(jnp.int32, (16, 128), 0)
    scale = jnp.where(row < 8, 0.5, jnp.where(row == 8, 0.25, 0.125))
    fields = fdot((summed * scale)[:, :96], expand)
    two, three = lanes_to_rows(fields[9:10], 8), lanes_to_rows(fields[8:9], 8)
    zero = jnp.zeros((8, 64), F32)
    upper = jnp.concatenate(
        [jnp.concatenate([three, zero], axis=1), jnp.concatenate([zero, two], axis=1)], axis=0
    )
    upper = fdot(upper, c("planes"), turned=True)
    four = fdot(lanes_to_rows(fields[:8], 8), c("pair_up"), turned=True)
    five = fdot(
        c("down"),
        jnp.concatenate([four, lanes_to_rows(upper[:8], 4), lanes_to_rows(upper[8:], 4)], axis=0),
    )
    results = []
    for q in range(8):
        part = five[q // 4 * 64 : q // 4 * 64 + 64, q % 4 * 64 : q % 4 * 64 + 64]
        results.append(rows_to_lanes(part, 8))
    return jnp.concatenate(results, axis=0)


def expand_five(summed, expand):
    parts = []
    for q in range(8):
        pz, lane = q // 4, 128 * (q % 4)
        parts.append(summed[8 * pz : 8 * pz + 8, lane : lane + 128])
    return fdot(jnp.concatenate(parts, axis=0)[:, :96], expand)


def down_five(result, lines, out_ref):
    for q in range(8):
        qz, qy, qx = octant(q)
        for lz in range(2):
            for ly in range(2):
                first = lz * 32 + qz * 16 + ly * 8 + qy * 4 + qx
                source = q * 8 + lz * 4 + ly * 2
                for n in range(4):
                    lines[n, pl.ds(first, 2, stride=2), :] = result[source : source + 2, 128 * n : 128 * n + 128]
    for n in range(4):
        out_ref[:, 128 * n : 128 * n + 128] = lines[n]


PAIRS = {"leaf_order": (64, 64), "spread": (128, 96), "pair_up": (256, 64)}
NARROW = {"lanes_five": 384, "lanes_four": 384, "back": 256}
SELECT = {"sel_three": 256, "sel_two": 128}


def places(sizes):
    start, found = 0, {}
    for name, rows in sizes.items():
        found[name] = start, rows
        start += -(-rows // 16) * 16
    return found, start


PAIR_PLACES, PAIR_ROWS = places({name: shape[0] for name, shape in PAIRS.items()})
NARROW_PLACES, NARROW_ROWS = places(NARROW)
SELECT_PLACES, SELECT_ROWS = places(SELECT)


def halved(value):
    value = value.astype(np.float32)
    high = value.astype(jnp.bfloat16)
    return np.stack([high, (value - high.astype(np.float32)).astype(jnp.bfloat16)])


def packed_tables(groups):
    t = tables()
    t["lanes_five"], t["lanes_four"] = t["lanes"]
    t["spread"] = t["spread"].T
    pairs = np.zeros((PAIR_ROWS, 128))
    for name, (start, rows) in PAIR_PLACES.items():
        pairs[start : start + rows, : PAIRS[name][1]] = t[name]
    narrow = np.zeros((NARROW_ROWS, 256))
    for name, (start, rows) in NARROW_PLACES.items():
        narrow[start : start + rows] = t[name]
    select = np.zeros((SELECT_ROWS, 512))
    for name, (start, rows) in SELECT_PLACES.items():
        select[start : start + rows] = t[name]
    short = lambda value: value.astype(jnp.bfloat16)
    return [
        halved(pairs), short(t["choose"]), short(t["gather"]), short(narrow), short(select),
        t["zmaps"], t["planes"], short(top_rows(groups // 4)), short(back_tops()),
    ]


def getter(pairs, gather, narrow, select, zmaps, planes):
    def get(name):
        if name in ("up", "down"):
            start = 0 if name == "up" else 2
            return zmaps[start], zmaps[start + 1]
        if name == "planes":
            return planes[0], planes[1]
        if name == "gather":
            return gather[0:256]
        if name == "shift":
            return gather[256:640]
        if name in PAIRS:
            start, rows = PAIR_PLACES[name]
            lanes = PAIRS[name][1]
            return tuple(pairs[half, start : start + rows, 0:lanes] for half in range(2))
        if name in NARROW:
            start, rows = NARROW_PLACES[name]
            return narrow[start : start + rows]
        start, rows = SELECT_PLACES[name]
        return select[start : start + rows]

    return get


def place_transfers(m2l, choose, weights, roll):
    for rank in range(0, 8, 2):
        if rank == 6:
            weights[:, 48:64, :] = jnp.zeros((49, 16, 256), BF16)
            continue
        sides = [[], []]
        for n in (rank, rank + 1):
            rows = jnp.concatenate([m2l[n], jnp.zeros((32, 316), BF16)], axis=0)
            low = bdot(choose[0:280, 0:256], rows[:, 0:256], turned=True)
            high = bdot(choose[280:392, 128:316], rows[:, 128:316], turned=True)
            value = jnp.concatenate([low, high], axis=0)
            sides[0].append(value.reshape(49, 8, 128))
            sides[1].append(roll(value, 1, 0).reshape(49, 8, 128))
        for px in range(2):
            both = jnp.concatenate(sides[px], axis=1).astype(BF16)
            weights[:, 8 * rank : 8 * rank + 16, 128 * px : 128 * px + 128] = both


def block_transfers(weights, pz, py, block):
    wz, wy = block // 3, block % 3
    cells = [(2 * wz + fz + 1 - pz) * 7 + 2 * wy + fy + 1 - py for fz in range(2) for fy in range(2)]
    return jnp.concatenate([weights[cell] for cell in cells], axis=0)


def far_tops(four, top_ref, weights, back_top):
    lefts = []
    for block in range(9):
        wz, wy = block // 3, block % 3
        fz_parts = [top_ref[16 * block + 8 * fz : 16 * block + 8 * fz + 8, :] for fz in range(2)]
        tops = jnp.concatenate([jnp.concatenate(fz_parts, axis=1), jnp.zeros((8, 256), F32)], axis=0)
        lefts.append(jnp.concatenate([four[wz, wy : wy + 2].reshape(32, 256), tops.astype(BF16)], axis=0))
    pieces = []
    for child in range(4):
        value = None
        for block in range(9):
            product = bdot(lefts[block], block_transfers(weights, child // 2, child % 2, block))
            value = product if value is None else value + product
        short = value.astype(BF16)
        pieces += [short[:, :128], short[:, 128:]]
    return bdot(back_top, jnp.concatenate(pieces, axis=0)).astype(BF16)


def far_five(five, weights, back, py):
    values = []
    for pz in range(2):
        value = None
        for block in range(9):
            wz, wy = block // 3, block % 3
            left = five[wz : wz + 2, wy : wy + 4].reshape(128, 256)
            product = bdot(left, block_transfers(weights, pz, py, block))
            value = product if value is None else value + product
        values.append(value.astype(BF16))
    return bdot(back, jnp.concatenate(values, axis=0)).astype(BF16)


DIRECTIONS = [(dz, dk) for dz in (-1, 0, 1) for dk in (-1, 0, 1) if (dz, dk) != (0, 0)]


def halo_ranges(step, size):
    if step == 0:
        return pl.ds(1, size), pl.ds(1, size)
    if step == 1:
        return pl.ds(size, 1), pl.ds(0, 1)
    return pl.ds(1, 1), pl.ds(size + 1, 1)


def kernel(groups, *refs):
    sources, out_ref, scratch = refs[:13], refs[13], refs[14:]
    (
        leaf, m2l, compress, expand, pairs, choose, gather, narrow, select, zmaps, planes, pick, back_top,
        weights, message, received, row_ref, raw, five, four, top_ref, reply_top, reply_five, answer_top, answer_five,
        lines, load, send_a, recv_a, send_t, recv_t, send_halo, recv_halo, send_d, recv_d,
    ) = scratch
    o, v = lax.axis_index("oct"), lax.axis_index("dev")
    gz, k, gy, gx = o // 4, o % 4, v // 8, v % 8
    roll = pltpu.roll
    c = getter(pairs, gather, narrow, select, zmaps, planes)

    loads = {}
    for n, target in enumerate(scratch[:13]):
        source = sources[n]
        if target is zmaps:
            source = source.at[gz % 2]
        if target is planes:
            source = source.at[gy % 2 * 2 + gx % 2]
        if target is pick:
            source = source.at[gz // 2 * 4 + k]
        if target is back_top:
            source = source.at[gz % 4 * 2 + k % 2]
        loads[n] = pltpu.make_async_copy(source, target, load.at[n])
    for n in (0, 4, 9, 10, 2):
        loads[n].start()

    raw[...] = jnp.zeros(raw.shape, BF16)
    barrier = pltpu.get_barrier_semaphore()
    layers = groups // 4
    partners = [(n, 0) for n in sorted(range(1, layers), key=lambda n: abs(n - layers // 2))] + [(0, n) for n in range(1, 4)]
    partners += [(dz % layers, dk % 4) for dz in (-1, 1) for dk in (-1, 1)]
    for dz, dk in partners:
        target = lax.rem(gz + dz, layers) * 4 + lax.rem(k + dk, 4)
        pl.semaphore_signal(barrier, inc=1, device_id=(target, v), device_id_type=MESH)
    for n in range(1, 16):
        pl.semaphore_signal(barrier, inc=1, device_id=(o, lax.rem(v + n, 16)), device_id_type=MESH)
    for n in (1, 5, 6, 7, 8, 11, 12, 3):
        loads[n].start()

    for n in (0, 4, 9, 10, 2):
        loads[n].wait()
    packed = upward(leaf[...], spread_ranks(compress[...], c), c)
    tiles = messages(packed, roll)
    for n in range(16):
        message[n] = tiles[n]
    received[v] = message[v]
    pl.semaphore_wait(barrier, 15 + len(partners))

    def across(source, target, sems, n):
        return pltpu.make_async_remote_copy(
            src_ref=source.at[lax.rem(v + n, 16)], dst_ref=target.at[v], send_sem=sems[0], recv_sem=sems[1],
            device_id=(o, lax.rem(v + n, 16)), device_id_type=MESH,
        )

    def along_k(n):
        return pltpu.make_async_remote_copy(
            src_ref=row_ref.at[pl.ds(o, 1)], dst_ref=row_ref.at[pl.ds(o, 1)],
            send_sem=send_t.at[0], recv_sem=recv_t.at[0],
            device_id=(gz * 4 + lax.rem(k + n, 4), v), device_id_type=MESH,
        )

    def along_z(n):
        return pltpu.make_async_remote_copy(
            src_ref=row_ref.at[pl.ds(gz * 4, 4)], dst_ref=row_ref.at[pl.ds(gz * 4, 4)],
            send_sem=send_t.at[1], recv_sem=recv_t.at[1],
            device_id=(lax.rem(gz + n, layers) * 4 + k, v), device_id_type=MESH,
        )

    def whole(source, target, count, sems):
        return pltpu.make_async_remote_copy(
            src_ref=source.at[pl.ds(0, count)], dst_ref=target.at[pl.ds(0, count)], send_sem=sems[0], recv_sem=sems[1],
            device_id=(o, lax.rem(v + 1, 16)), device_id_type=MESH,
        )

    sems_a = (send_a, recv_a)
    for n in range(1, 16):
        across(message, received, sems_a, n).start()
    for n in (1, 5, 6, 7, 8, 11, 12, 3):
        loads[n].wait()
    place_transfers(m2l, choose, weights, roll)
    whole(message, received, 15, sems_a).wait_recv()

    got = [received[n] for n in range(16)]
    row_ref[o] = top_row(got, roll)
    for n in range(1, 4):
        along_k(n).start()
    raw[1:3, 1:5] = assemble(jnp.concatenate(got, axis=0), c).reshape(2, 4, 16, 128)

    def halo(number, dz, dk, sign):
        from_z, to_z = halo_ranges(dz, 2)
        from_y, to_y = halo_ranges(dk, 4)
        return pltpu.make_async_remote_copy(
            src_ref=raw.at[from_z, from_y], dst_ref=raw.at[to_z, to_y],
            send_sem=send_halo.at[number], recv_sem=recv_halo.at[number],
            device_id=((gz + sign * dz) * 4 + k + sign * dk, v), device_id_type=MESH,
        )

    def inside(dz, dk):
        return (gz + dz >= 0) & (gz + dz < groups // 4) & (k + dk >= 0) & (k + dk < 4)

    for number, (dz, dk) in enumerate(DIRECTIONS):
        @pl.when(inside(dz, dk))
        def _():
            halo(number, dz, dk, 1).start()

    def rows_of(step):
        return whole(row_ref, row_ref, (3, groups - 4)[step], (send_t.at[step], recv_t.at[step]))

    rows_of(0).wait_recv()
    for n in range(1, layers):
        along_z(n).start()

    widen(raw, OWN, five, four, c)

    for number, (dz, dk) in enumerate(DIRECTIONS):
        @pl.when(inside(-dz, -dk))
        def _():
            halo(number, dz, dk, -1).wait_recv()

    widen(raw, AROUND, five, four, c)
    returned = [(reply_five.at[n], answer_five.at[n], (send_d.at[n], recv_d.at[n])) for n in range(2)]
    returned_top = (reply_top, answer_top, (send_d.at[2], recv_d.at[2]))

    def half(py):
        reply_five[py] = far_five(five, weights, c("back"), py).reshape(16, 16, 256)
        answer_five[py, v] = reply_five[py, v]
        for n in range(1, 16):
            across(*returned[py], n).start()

    half(0)
    rows_of(1).wait_recv()
    rows = [row_ref[n] for n in range(groups)]
    top_ref[...] = top_blocks(rows, pick[...], c)
    reply_top[...] = far_tops(four, top_ref, weights, back_top[...]).reshape(16, 16, 128)
    answer_top[v] = reply_top[v]
    for n in range(1, 16):
        across(*returned_top, n).start()
    half(1)

    split_expand = split(expand[...])
    whole(message, received, 15, sems_a).wait_send()
    for number, (dz, dk) in enumerate(DIRECTIONS):
        @pl.when(inside(dz, dk))
        def _():
            halo(number, dz, dk, 1).wait_send()

    whole(*returned_top[:2], 15, returned_top[2]).wait_recv()
    above = down_top(lift_up(answer_top), split_expand, c)
    halves = []
    for py in range(2):
        whole(*returned[py][:2], 15, returned[py][2]).wait_recv()
        halves.append(lift_up(answer_five.at[py]))
    low = expand_five(jnp.concatenate(halves, axis=1), split_expand)
    down_five(low + above, lines, out_ref)
    for source, target, sems in (*returned, returned_top):
        whole(source, target, 15, sems).wait_send()
    for step in range(2):
        rows_of(step).wait_send()


def on_device(groups, leaf_multipoles, m2l_ops, compress, expand):
    values = [leaf_multipoles, m2l_ops.transpose(1, 2, 0), compress.T, expand]
    values += [jnp.asarray(value) for value in packed_tables(groups)]
    dma = pltpu.SemaphoreType.DMA
    loaded = [pltpu.VMEM(value.shape, value.dtype) for value in values[:-4]]
    loaded += [pltpu.VMEM(value.shape[1:], value.dtype) for value in values[-4:]]
    return pl.pallas_call(
        lambda *refs: kernel(groups, *refs),
        out_shape=jax.ShapeDtypeStruct((64, 512), F32),
        in_specs=[pl.BlockSpec(memory_space=pltpu.HBM)] * len(values),
        out_specs=pl.BlockSpec(memory_space=pltpu.VMEM),
        scratch_shapes=loaded
        + [
            pltpu.VMEM((49, 64, 256), BF16),
            pltpu.VMEM((16, 8, 128), F32),
            pltpu.VMEM((16, 8, 128), F32),
            pltpu.VMEM((groups, 1, 384), F32),
            pltpu.VMEM((4, 6, 16, 128), BF16),
            pltpu.VMEM((4, 6, 16, 256), BF16),
            pltpu.VMEM((3, 4, 16, 256), BF16),
            pltpu.VMEM((144, 128), F32),
            pltpu.VMEM((16, 16, 128), BF16),
            pltpu.VMEM((2, 16, 16, 256), BF16),
            pltpu.VMEM((16, 16, 128), BF16),
            pltpu.VMEM((2, 16, 16, 256), BF16),
            pltpu.VMEM((4, 64, 128), F32),
            dma((13,)),
            dma, dma, dma((2,)), dma((2,)), dma((8,)), dma((8,)), dma((3,)), dma((3,)),
        ],
        compiler_params=pltpu.CompilerParams(
            collective_id=0, has_side_effects=True, vmem_limit_bytes=55000 * 1024
        ),
        cost_estimate=pl.CostEstimate(flops=1_000_000_000, bytes_accessed=6_000_000, transcendentals=0),
    )(*values)


def solution(mesh):
    groups = mesh.shape["oct"]
    placed = (P(("oct", "dev"), None), P(None, "dev", None), P(), P())
    return jax.shard_map(
        lambda *args: on_device(groups, *args),
        mesh=mesh, in_specs=placed, out_specs=P(("oct", "dev"), None), check_vma=False,
    )
```

```python
import math

import jax
import jax.numpy as jnp
import numpy as np
from jax import lax
from jax.experimental import pallas as pl
from jax.experimental.pallas import tpu as pltpu
from jax.sharding import PartitionSpec as P


F32 = jnp.float32
BF16 = jnp.bfloat16
MESH = pl.DeviceIdType.MESH
TOPS = 48


def side_maps():
    ids = np.arange(8, dtype=np.float64)
    angles = (2 * ids + 1) * math.pi / 16
    points = np.cos(angles)
    degrees = np.arange(1, 8, dtype=np.float64)
    parent = np.cos(angles[:, None] * degrees[None, :])
    maps = []
    for side in range(2):
        child = np.cos(np.arccos((points + 2 * side - 1) / 2)[:, None] * degrees[None, :])
        maps.append(1 / 8 + 2 / 8 * parent @ child.T)
    return np.stack(maps)


def octant(number):
    return number // 4, number // 2 % 2, number % 2


def tables():
    side = side_maps()
    t = {}
    leaf_order = np.zeros((64, 64))
    up_five = np.zeros((8, 8, 8, 2, 8))
    for box in range(64):
        a, b, c = box // 16, box // 4 % 4, box % 4
        parent = (a // 2) * 4 + (b // 2) * 2 + c // 2
        leaf_order[((b % 2) * 2 + c % 2) * 16 + (a % 2) * 8 + parent, box] = 1
        up_five[:, parent, :, a % 2, parent] = side[a % 2]
    t["leaf_order"] = leaf_order
    pair = np.zeros((2, 2, 8, 8, 8, 8))
    for qy in range(2):
        for qx in range(2):
            pair[qy, qx] = np.einsum("ab,cd->bdac", side[qy], side[qx])
    t["pair_up"] = pair.reshape(256, 64)
    twice = np.stack([side[a // 2] @ side[a % 2] for a in range(4)])
    zmaps, planes = [], []
    for own in range(2):
        upper = np.stack([twice, side[own] @ twice])
        up = np.zeros((2, 4, 8, 8, 2, 8))
        down = np.zeros((2, 8, 8, 128))
        for box in range(8):
            lz, rest = box // 4, box % 4
            for qz in range(2):
                for level in range(2):
                    up[level, rest, :, :, qz, box] = upper[level, 2 * lz + qz]
                    start = 64 + 32 * level + 8 * rest
                    down[qz, :, box, start : start + 8] = upper[level, 2 * lz + qz].T
                for node in range(8):
                    down[qz, :, box, node * 8 + box] = side[qz][node]
        up = np.concatenate([up_five.reshape(64, 128), up.reshape(64, 128)])
        zmaps.append(np.concatenate([halved(up), halved(down.reshape(128, 128))]))
    for own in range(4):
        plane = np.zeros((2, 2, 2, 2, 8, 8, 2, 8, 8))
        for ly, lx, qy, qx in np.ndindex(2, 2, 2, 2):
            first, second = twice[2 * ly + qy], twice[2 * lx + qx]
            plane[ly, lx, qy, qx, :, :, 0] = np.einsum("ab,cd->bdac", first, second)
            plane[ly, lx, qy, qx, :, :, 1] = np.einsum("ab,cd->bdac", side[own // 2] @ first, side[own % 2] @ second)
        planes.append(halved(plane.reshape(1024, 128)))
    t["zmaps"] = np.stack(zmaps)
    t["planes"] = np.stack(planes)
    spread = np.zeros((96, 128))
    for rank in range(96):
        spread[rank, rank // 6 * 8 + rank % 6] = 1
    t["spread"] = spread
    gather = np.zeros((2, 2, 4, 16, 128))
    shift = np.zeros((3, 8, 16, 8, 16))
    lanes = np.zeros((2, 3, 128, 256))
    for pz in range(2):
        for py in range(4):
            for px in range(16):
                source = (py // 2) * 8 + px // 2
                gather[0, pz, py, px, source * 8 + pz * 4 + (py % 2) * 2 + px % 2] = 1
                if py in (0, 3) and px < 8:
                    gather[1, pz, py, px, ((py == 3) * 8 + px) * 8] = 1
    for wx in range(3):
        for px in range(16):
            if 0 <= px + wx - 1 < 16:
                for block in range(8):
                    shift[wx, block, px, block, px + wx - 1] = 1
        for phase in range(8):
            for r in range(8):
                place = phase // 2 * 64 + r * 8 + 1 + 2 * wx + phase % 2
                lanes[0, wx, phase * 8 + r, place] = 1
                lanes[1, wx, 64 + phase * 8 + r, place] = 1
    t["gather"] = np.concatenate([gather.reshape(256, 128), shift.reshape(384, 128)])
    t["lanes"] = lanes.reshape(2, 384, 256)
    sel_three = np.zeros((256, 512))
    for gy in range(2):
        for px in range(4):
            for node in range(1, 7):
                gx = 2 * px - 3 + node
                if 0 <= gx < 8:
                    for r in range(8):
                        sel_three[gy * 128 + 64 + gx * 8 + r, px * 128 + gy * 64 + r * 8 + node] = 1
    t["sel_three"] = sel_three
    sel_two = np.zeros((128, 512))
    for px in range(2):
        for fy in range(2):
            for node in range(1, 7):
                bx = 2 * px - 3 + node
                if 0 <= bx < 4:
                    for r in range(8):
                        sel_two[64 + bx * 8 + r, (px * 2 + fy) * 128 + fy * 64 + r * 8 + node] = 1
    t["sel_two"] = sel_two
    back = np.zeros((16, 16, 256))
    for source in range(16):
        for lp in range(8):
            lz, ly, lx = octant(lp)
            row = lz * 64 + ((source // 8) * 2 + ly) * 16 + (source % 8) * 2 + lx
            back[source, lp, row] = 1
            back[source, 8 + lp, 128 + row] = 1
    t["back"] = back.reshape(256, 256)
    choose = np.zeros((49, 8, 316))
    number = 0
    for cell in range(49):
        for x in range(7):
            if max(abs(cell // 7 - 3), abs(cell % 7 - 3), abs(x - 3)) > 1:
                choose[cell, x, number] = 1
                number += 1
    t["choose"] = choose.reshape(392, 316)
    return t


def top_rows(levels_z):
    table = np.zeros((levels_z // 2, 4, 9, 2, 8, 256))
    for half in range(levels_z // 2):
        for k in range(4):
            for block in range(9):
                for fz in range(2):
                    z = 2 * (half + block // 3 - 1) + fz
                    y = k + block % 3 - 1
                    if 0 <= z < levels_z and 0 <= y < 4:
                        for px in range(4):
                            table[half, k, block, fz, px, px * 32 + z * 4 + y] = 1
                    z = 2 * (half // 2 + block // 3 - 1) + fz
                    for fy in range(2):
                        y = 2 * (k // 2 + block % 3 - 1) + fy
                        if 0 <= z < levels_z // 2 and 0 <= y < 4:
                            for px in range(2):
                                table[half, k, block, fz, 4 + px, 128 + (px * 2 + fy) * 16 + z * 4 + y] = 1
    return table.reshape(levels_z // 2 * 4, 144, 256)[:, :, :192]


def back_tops():
    table = np.zeros((4, 2, 16, 16, 8, TOPS))
    for gz in range(4):
        for k in range(2):
            for source in range(16):
                gy, gx = source // 8, source % 8
                for q in range(8):
                    table[gz, k, source, q, q, gy * 16 + gx] = 1
                table[gz, k, source, 8, gz % 2 * 4 + gy * 2 + gx % 2, 32 + gx // 2] = 1
                table[gz, k, source, 9, gz // 2 * 4 + k * 2 + gx // 2 % 2, 36 + gx // 4] = 1
    return table.reshape(8, 256, 8 * TOPS)


def split(value):
    if isinstance(value, tuple):
        return value
    high = value.astype(BF16)
    return high, (value - high.astype(F32)).astype(BF16)


def fdot(a, b, turned=False):
    (a_high, a_low), (b_high, b_low) = split(a), split(b)
    return bdot(a_high, b_high, turned) + (bdot(a_high, b_low, turned) + bdot(a_low, b_high, turned))


def bdot(a, b, turned=False):
    return lax.dot_general(a, b, (((1,), (1 if turned else 0,)), ((), ())), preferred_element_type=F32)


def rows_to_lanes(value, count):
    rows = value.shape[0] // count
    return jnp.concatenate([value[rows * n : rows * n + rows] for n in range(count)], axis=1)


def lanes_to_rows(value, count):
    width = value.shape[1] // count
    return jnp.concatenate([value[:, width * n : width * n + width] for n in range(count)], axis=0)


def upward(leaves, spread, c):
    order = c("leaf_order")[0]
    parts = [bdot(order, part) for part in split(leaves)]
    mixed = []
    for part in parts:
        lines = []
        for node in range(8):
            lines.append(
                jnp.concatenate([part[16 * n : 16 * n + 16, 64 * node : 64 * node + 64] for n in range(4)], axis=1)
            )
        mixed.append(jnp.concatenate(lines, axis=0).astype(BF16))
    mixed = fdot(c("up"), tuple(mixed))
    four = fdot(mixed[:64], c("pair_up"))
    upper = jnp.concatenate([rows_to_lanes(mixed[64:96], 4), rows_to_lanes(mixed[96:], 4)], axis=0)
    upper = fdot(upper, c("planes"))
    three, two = upper[:8, :64], upper[8:, 64:]
    rest = jnp.concatenate(
        [rows_to_lanes(four, 8), rows_to_lanes(three, 8), rows_to_lanes(two, 8), jnp.zeros((6, 512), F32)], axis=0
    )
    every = [jnp.concatenate([part.astype(BF16), extra], axis=0) for part, extra in zip(parts, split(rest))]
    return fdot(tuple(every), spread, turned=True)


def spread_ranks(turned_compress, c):
    return tuple(bdot(c("spread")[0], part).astype(BF16) for part in split(turned_compress))


def messages(packed, roll):
    tiles = []
    for q in range(8):
        first = q % 4 * 16 + q // 4 * 8
        tiles.append(packed[first : first + 8])
    for q in range(8):
        lines = [packed[64 + q : 65 + q]] + ([packed[72:73], packed[73:74]] if q == 0 else [])
        tiles.append(jnp.concatenate(lines + [jnp.zeros((8 - len(lines), 128), F32)], axis=0))
    lane = lax.broadcasted_iota(jnp.int32, (8, 128), 1)
    for bit in (1, 2, 4, 8):
        upper = lane // 8 // bit % 2 == 1
        for n in range(16):
            if n & bit == 0:
                low, high = tiles[n], tiles[n | bit]
                tiles[n] = jnp.where(upper, roll(high, 8 * bit, 1), low)
                tiles[n | bit] = jnp.where(upper, high, roll(low, 128 - 8 * bit, 1))
    return tiles


def top_row(tiles, roll):
    lane = lax.broadcasted_iota(jnp.int32, (8, 128), 1)
    mask = lane // 8 == 8
    sums = [jnp.zeros((8, 128), F32) for _ in range(3)]
    for n in range(16):
        kept = jnp.where(mask, tiles[n], 0.0)
        gx = n % 8
        sums[n // 8] += roll(kept, 8 * gx, 1) if gx else kept
        sums[2] += roll(kept, 8 * (gx // 2), 1) if gx // 2 else kept
    return jnp.concatenate([sums[0][1:2], sums[1][1:2], sums[2][2:3]], axis=1)


def assemble(received, c):
    picked = bdot(c("gather"), received.astype(BF16))
    lane = lax.broadcasted_iota(jnp.int32, (128, 128), 1)
    return jnp.where(lane < 64, picked[:128], picked[128:]).astype(BF16)


def widen(raw, blocks, five, four, c):
    narrow = jnp.concatenate([raw[z, y] for z, y in blocks], axis=0)
    wide, fours = [], []
    for start in range(0, len(blocks), 8):
        shifted = bdot(c("shift"), narrow[16 * start : 16 * start + 128]).astype(BF16)
        wide.append(rows_to_lanes(shifted, 3))
    wide = jnp.concatenate(wide, axis=0)
    result = bdot(wide, c("lanes_five")).astype(BF16)
    for n, (z, y) in enumerate(blocks):
        five[z, y] = result[16 * n : 16 * n + 16]
        if z in (0, 1, 3) and y in (0, 1, 4, 5):
            fours.append((n, (0, 1, 3).index(z), (0, 1, 4, 5).index(y)))
    result = bdot(jnp.concatenate([wide[16 * n : 16 * n + 16] for n, _, _ in fours], axis=0), c("lanes_four"))
    for place, (_, z, y) in enumerate(fours):
        four[z, y] = result[16 * place : 16 * place + 16].astype(BF16)


OWN = [(z, y) for z in (1, 2) for y in range(1, 5)]
AROUND = [(z, y) for z in range(4) for y in range(6) if (z, y) not in OWN]


def top_blocks(rows, pick, c):
    three = jnp.concatenate([row[:, :256] for row in rows], axis=0).astype(BF16)
    pairs = []
    for n in range(16):
        first = n // 4 * 8 + n % 4
        pairs.append(rows[first][:, 256:] + rows[first + 4][:, 256:])
    two = jnp.concatenate(pairs, axis=0).astype(BF16)
    stacked = jnp.concatenate(
        [
            lanes_to_rows(bdot(three, c("sel_three")), 4),
            lanes_to_rows(bdot(two, c("sel_two")), 4),
        ],
        axis=0,
    ).astype(BF16)
    return bdot(pick, stacked)


def lift_up(summed):
    total = summed[0].astype(F32)
    for n in range(1, 16):
        total = total + summed[n].astype(F32)
    return total


def down_top(summed, expand, c):
    row = lax.broadcasted_iota(jnp.int32, (16, 128), 0)
    scale = jnp.where(row < 8, 0.5, jnp.where(row == 8, 0.25, 0.125))
    fields = fdot((summed * scale)[:, :96], expand)
    two, three = lanes_to_rows(fields[9:10], 8), lanes_to_rows(fields[8:9], 8)
    zero = jnp.zeros((8, 64), F32)
    upper = jnp.concatenate(
        [jnp.concatenate([three, zero], axis=1), jnp.concatenate([zero, two], axis=1)], axis=0
    )
    upper = fdot(upper, c("planes"), turned=True)
    four = fdot(lanes_to_rows(fields[:8], 8), c("pair_up"), turned=True)
    five = fdot(
        c("down"),
        jnp.concatenate([four, lanes_to_rows(upper[:8], 4), lanes_to_rows(upper[8:], 4)], axis=0),
    )
    results = []
    for q in range(8):
        part = five[q // 4 * 64 : q // 4 * 64 + 64, q % 4 * 64 : q % 4 * 64 + 64]
        results.append(rows_to_lanes(part, 8))
    return jnp.concatenate(results, axis=0)


def expand_five(summed, expand):
    parts = []
    for q in range(8):
        pz, lane = q // 4, 128 * (q % 4)
        parts.append(summed[8 * pz : 8 * pz + 8, lane : lane + 128])
    return fdot(jnp.concatenate(parts, axis=0)[:, :96], expand)


def down_five(result, lines, out_ref):
    for q in range(8):
        qz, qy, qx = octant(q)
        for lz in range(2):
            for ly in range(2):
                first = lz * 32 + qz * 16 + ly * 8 + qy * 4 + qx
                source = q * 8 + lz * 4 + ly * 2
                for n in range(4):
                    lines[n, pl.ds(first, 2, stride=2), :] = result[source : source + 2, 128 * n : 128 * n + 128]
    for n in range(4):
        out_ref[:, 128 * n : 128 * n + 128] = lines[n]


PAIRS = {"leaf_order": (64, 64), "spread": (128, 96), "pair_up": (256, 64)}
NARROW = {"lanes_five": 384, "lanes_four": 384, "back": 256}
SELECT = {"sel_three": 256, "sel_two": 128}


def places(sizes):
    start, found = 0, {}
    for name, rows in sizes.items():
        found[name] = start, rows
        start += -(-rows // 16) * 16
    return found, start


PAIR_PLACES, PAIR_ROWS = places({name: shape[0] for name, shape in PAIRS.items()})
NARROW_PLACES, NARROW_ROWS = places(NARROW)
SELECT_PLACES, SELECT_ROWS = places(SELECT)


def halved(value):
    value = value.astype(np.float32)
    high = value.astype(jnp.bfloat16)
    return np.stack([high, (value - high.astype(np.float32)).astype(jnp.bfloat16)])


def packed_tables(groups):
    t = tables()
    t["lanes_five"], t["lanes_four"] = t["lanes"]
    t["spread"] = t["spread"].T
    pairs = np.zeros((PAIR_ROWS, 128))
    for name, (start, rows) in PAIR_PLACES.items():
        pairs[start : start + rows, : PAIRS[name][1]] = t[name]
    narrow = np.zeros((NARROW_ROWS, 256))
    for name, (start, rows) in NARROW_PLACES.items():
        narrow[start : start + rows] = t[name]
    select = np.zeros((SELECT_ROWS, 512))
    for name, (start, rows) in SELECT_PLACES.items():
        select[start : start + rows] = t[name]
    short = lambda value: value.astype(jnp.bfloat16)
    return [
        halved(pairs), short(t["choose"]), short(t["gather"]), short(narrow), short(select),
        t["zmaps"], t["planes"], short(top_rows(groups // 4)), short(back_tops()),
    ]


def getter(pairs, gather, narrow, select, zmaps, planes):
    def get(name):
        if name in ("up", "down"):
            start = 0 if name == "up" else 2
            return zmaps[start], zmaps[start + 1]
        if name == "planes":
            return planes[0], planes[1]
        if name == "gather":
            return gather[0:256]
        if name == "shift":
            return gather[256:640]
        if name in PAIRS:
            start, rows = PAIR_PLACES[name]
            lanes = PAIRS[name][1]
            return tuple(pairs[half, start : start + rows, 0:lanes] for half in range(2))
        if name in NARROW:
            start, rows = NARROW_PLACES[name]
            return narrow[start : start + rows]
        start, rows = SELECT_PLACES[name]
        return select[start : start + rows]

    return get


def place_transfers(m2l, choose, weights, roll):
    for rank in range(0, 8, 2):
        if rank == 6:
            weights[:, 48:64, :] = jnp.zeros((49, 16, 256), BF16)
            continue
        sides = [[], []]
        for n in (rank, rank + 1):
            rows = jnp.concatenate([m2l[n], jnp.zeros((32, 316), BF16)], axis=0)
            low = bdot(choose[0:280, 0:256], rows[:, 0:256], turned=True)
            high = bdot(choose[280:392, 128:316], rows[:, 128:316], turned=True)
            value = jnp.concatenate([low, high], axis=0)
            sides[0].append(value.reshape(49, 8, 128))
            sides[1].append(roll(value, 1, 0).reshape(49, 8, 128))
        for px in range(2):
            both = jnp.concatenate(sides[px], axis=1).astype(BF16)
            weights[:, 8 * rank : 8 * rank + 16, 128 * px : 128 * px + 128] = both


def block_transfers(weights, pz, py, block):
    wz, wy = block // 3, block % 3
    cells = [(2 * wz + fz + 1 - pz) * 7 + 2 * wy + fy + 1 - py for fz in range(2) for fy in range(2)]
    return jnp.concatenate([weights[cell] for cell in cells], axis=0)


def far_tops(four, top_ref, weights, back_top):
    lefts = []
    for block in range(9):
        wz, wy = block // 3, block % 3
        fz_parts = [top_ref[16 * block + 8 * fz : 16 * block + 8 * fz + 8, :] for fz in range(2)]
        tops = jnp.concatenate([jnp.concatenate(fz_parts, axis=1), jnp.zeros((8, 256), F32)], axis=0)
        lefts.append(jnp.concatenate([four[wz, wy : wy + 2].reshape(32, 256), tops.astype(BF16)], axis=0))
    pieces = []
    for child in range(4):
        value = None
        for block in range(9):
            product = bdot(lefts[block], block_transfers(weights, child // 2, child % 2, block))
            value = product if value is None else value + product
        short = value.astype(BF16)
        pieces += [short[:, :128], short[:, 128:]]
    return bdot(back_top, jnp.concatenate(pieces, axis=0)).astype(BF16)


def far_five(five, weights, back, py):
    values = []
    for pz in range(2):
        value = None
        for block in range(9):
            wz, wy = block // 3, block % 3
            left = five[wz : wz + 2, wy : wy + 4].reshape(128, 256)
            product = bdot(left, block_transfers(weights, pz, py, block))
            value = product if value is None else value + product
        values.append(value.astype(BF16))
    return bdot(back, jnp.concatenate(values, axis=0)).astype(BF16)


DIRECTIONS = [(dz, dk) for dz in (-1, 0, 1) for dk in (-1, 0, 1) if (dz, dk) != (0, 0)]


def halo_ranges(step, size):
    if step == 0:
        return pl.ds(1, size), pl.ds(1, size)
    if step == 1:
        return pl.ds(size, 1), pl.ds(0, 1)
    return pl.ds(1, 1), pl.ds(size + 1, 1)


def kernel(groups, *refs):
    sources, out_ref, scratch = refs[:13], refs[13], refs[14:]
    (
        leaf, m2l, compress, expand, pairs, choose, gather, narrow, select, zmaps, planes, pick, back_top,
        weights, message, received, row_ref, raw, five, four, top_ref, reply_top, reply_five, answer_top, answer_five,
        lines, load, send_a, recv_a, send_t, recv_t, send_halo, recv_halo, send_d, recv_d,
    ) = scratch
    o, v = lax.axis_index("oct"), lax.axis_index("dev")
    gz, k, gy, gx = o // 4, o % 4, v // 8, v % 8
    roll = pltpu.roll
    c = getter(pairs, gather, narrow, select, zmaps, planes)

    loads = {}
    for n, target in enumerate(scratch[:13]):
        source = sources[n]
        if target is zmaps:
            source = source.at[gz % 2]
        if target is planes:
            source = source.at[gy % 2 * 2 + gx % 2]
        if target is pick:
            source = source.at[gz // 2 * 4 + k]
        if target is back_top:
            source = source.at[gz % 4 * 2 + k % 2]
        loads[n] = pltpu.make_async_copy(source, target, load.at[n])
    for n in (0, 4, 9, 10, 2):
        loads[n].start()

    raw[...] = jnp.zeros(raw.shape, BF16)
    barrier = pltpu.get_barrier_semaphore()
    layers = groups // 4
    partners = [(n, 0) for n in sorted(range(1, layers), key=lambda n: abs(n - layers // 2))] + [(0, n) for n in range(1, 4)]
    partners += [(dz % layers, dk % 4) for dz in (-1, 1) for dk in (-1, 1)]
    for dz, dk in partners:
        target = lax.rem(gz + dz, layers) * 4 + lax.rem(k + dk, 4)
        pl.semaphore_signal(barrier, inc=1, device_id=(target, v), device_id_type=MESH)
    for n in range(1, 16):
        pl.semaphore_signal(barrier, inc=1, device_id=(o, lax.rem(v + n, 16)), device_id_type=MESH)
    for n in (1, 5, 6, 7, 8, 11, 12, 3):
        loads[n].start()

    for n in (0, 4, 9, 10, 2):
        loads[n].wait()
    packed = upward(leaf[...], spread_ranks(compress[...], c), c)
    tiles = messages(packed, roll)
    for n in range(16):
        message[n] = tiles[n]
    received[v] = message[v]
    pl.semaphore_wait(barrier, 15 + len(partners))

    def across(source, target, sems, n):
        return pltpu.make_async_remote_copy(
            src_ref=source.at[lax.rem(v + n, 16)], dst_ref=target.at[v], send_sem=sems[0], recv_sem=sems[1],
            device_id=(o, lax.rem(v + n, 16)), device_id_type=MESH,
        )

    def along_k(n):
        return pltpu.make_async_remote_copy(
            src_ref=row_ref.at[pl.ds(o, 1)], dst_ref=row_ref.at[pl.ds(o, 1)],
            send_sem=send_t.at[0], recv_sem=recv_t.at[0],
            device_id=(gz * 4 + lax.rem(k + n, 4), v), device_id_type=MESH,
        )

    def along_z(n):
        return pltpu.make_async_remote_copy(
            src_ref=row_ref.at[pl.ds(gz * 4, 4)], dst_ref=row_ref.at[pl.ds(gz * 4, 4)],
            send_sem=send_t.at[1], recv_sem=recv_t.at[1],
            device_id=(lax.rem(gz + n, layers) * 4 + k, v), device_id_type=MESH,
        )

    def whole(source, target, count, sems):
        return pltpu.make_async_remote_copy(
            src_ref=source.at[pl.ds(0, count)], dst_ref=target.at[pl.ds(0, count)], send_sem=sems[0], recv_sem=sems[1],
            device_id=(o, lax.rem(v + 1, 16)), device_id_type=MESH,
        )

    sems_a = (send_a, recv_a)
    for n in range(1, 16):
        across(message, received, sems_a, n).start()
    for n in (1, 5, 6, 7, 8, 11, 12, 3):
        loads[n].wait()
    place_transfers(m2l, choose, weights, roll)
    whole(message, received, 15, sems_a).wait_recv()

    got = [received[n] for n in range(16)]
    row_ref[o] = top_row(got, roll)
    for n in range(1, 4):
        along_k(n).start()
    raw[1:3, 1:5] = assemble(jnp.concatenate(got, axis=0), c).reshape(2, 4, 16, 128)

    def halo(number, dz, dk, sign):
        from_z, to_z = halo_ranges(dz, 2)
        from_y, to_y = halo_ranges(dk, 4)
        return pltpu.make_async_remote_copy(
            src_ref=raw.at[from_z, from_y], dst_ref=raw.at[to_z, to_y],
            send_sem=send_halo.at[number], recv_sem=recv_halo.at[number],
            device_id=((gz + sign * dz) * 4 + k + sign * dk, v), device_id_type=MESH,
        )

    def inside(dz, dk):
        return (gz + dz >= 0) & (gz + dz < groups // 4) & (k + dk >= 0) & (k + dk < 4)

    def rows_of(step):
        return whole(row_ref, row_ref, (3, groups - 4)[step], (send_t.at[step], recv_t.at[step]))

    rows_of(0).wait_recv()
    for n in range(1, layers):
        along_z(n).start()

    for number, (dz, dk) in enumerate(DIRECTIONS):
        @pl.when(inside(dz, dk))
        def _():
            halo(number, dz, dk, 1).start()

    widen(raw, OWN, five, four, c)

    for number, (dz, dk) in enumerate(DIRECTIONS):
        @pl.when(inside(-dz, -dk))
        def _():
            halo(number, dz, dk, -1).wait_recv()

    widen(raw, AROUND, five, four, c)
    returned = [(reply_five.at[n], answer_five.at[n], (send_d.at[n], recv_d.at[n])) for n in range(2)]
    returned_top = (reply_top, answer_top, (send_d.at[2], recv_d.at[2]))

    def half(py):
        reply_five[py] = far_five(five, weights, c("back"), py).reshape(16, 16, 256)
        answer_five[py, v] = reply_five[py, v]
        for n in range(1, 16):
            across(*returned[py], n).start()

    half(0)
    rows_of(1).wait_recv()
    rows = [row_ref[n] for n in range(groups)]
    top_ref[...] = top_blocks(rows, pick[...], c)
    reply_top[...] = far_tops(four, top_ref, weights, back_top[...]).reshape(16, 16, 128)
    answer_top[v] = reply_top[v]
    for n in range(1, 16):
        across(*returned_top, n).start()
    half(1)

    split_expand = split(expand[...])
    whole(message, received, 15, sems_a).wait_send()
    for number, (dz, dk) in enumerate(DIRECTIONS):
        @pl.when(inside(dz, dk))
        def _():
            halo(number, dz, dk, 1).wait_send()

    whole(*returned_top[:2], 15, returned_top[2]).wait_recv()
    above = down_top(lift_up(answer_top), split_expand, c)
    halves = []
    for py in range(2):
        whole(*returned[py][:2], 15, returned[py][2]).wait_recv()
        halves.append(lift_up(answer_five.at[py]))
    low = expand_five(jnp.concatenate(halves, axis=1), split_expand)
    down_five(low + above, lines, out_ref)
    for source, target, sems in (*returned, returned_top):
        whole(source, target, 15, sems).wait_send()
    for step in range(2):
        rows_of(step).wait_send()


def on_device(groups, leaf_multipoles, m2l_ops, compress, expand):
    values = [leaf_multipoles, m2l_ops.transpose(1, 2, 0), compress.T, expand]
    values += [jnp.asarray(value) for value in packed_tables(groups)]
    dma = pltpu.SemaphoreType.DMA
    loaded = [pltpu.VMEM(value.shape, value.dtype) for value in values[:-4]]
    loaded += [pltpu.VMEM(value.shape[1:], value.dtype) for value in values[-4:]]
    return pl.pallas_call(
        lambda *refs: kernel(groups, *refs),
        out_shape=jax.ShapeDtypeStruct((64, 512), F32),
        in_specs=[pl.BlockSpec(memory_space=pltpu.HBM)] * len(values),
        out_specs=pl.BlockSpec(memory_space=pltpu.VMEM),
        scratch_shapes=loaded
        + [
            pltpu.VMEM((49, 64, 256), BF16),
            pltpu.VMEM((16, 8, 128), F32),
            pltpu.VMEM((16, 8, 128), F32),
            pltpu.VMEM((groups, 1, 384), F32),
            pltpu.VMEM((4, 6, 16, 128), BF16),
            pltpu.VMEM((4, 6, 16, 256), BF16),
            pltpu.VMEM((3, 4, 16, 256), BF16),
            pltpu.VMEM((144, 128), F32),
            pltpu.VMEM((16, 16, 128), BF16),
            pltpu.VMEM((2, 16, 16, 256), BF16),
            pltpu.VMEM((16, 16, 128), BF16),
            pltpu.VMEM((2, 16, 16, 256), BF16),
            pltpu.VMEM((4, 64, 128), F32),
            dma((13,)),
            dma, dma, dma((2,)), dma((2,)), dma((8,)), dma((8,)), dma((3,)), dma((3,)),
        ],
        compiler_params=pltpu.CompilerParams(
            collective_id=0, has_side_effects=True, vmem_limit_bytes=55000 * 1024
        ),
        cost_estimate=pl.CostEstimate(flops=1_000_000_000, bytes_accessed=6_000_000, transcendentals=0),
    )(*values)


def solution(mesh):
    groups = mesh.shape["oct"]
    placed = (P(("oct", "dev"), None), P(None, "dev", None), P(), P())
    return jax.shard_map(
        lambda *args: on_device(groups, *args),
        mesh=mesh, in_specs=placed, out_specs=P(("oct", "dev"), None), check_vma=False,
    )
```
